512 devices in a mesh: seq: 128 (over x, y, z_lo), head: 4 (over z_hi, core).
Axes of the slice: x: 4, y: 4, z: 16 (z_hi: 2, z_lo: 8; z = z_hi * 8 + z_lo), core: 2. Of those that a mesh axis runs over, the one named last changes fastest.
Arguments:
- tokens: bfloat16 [24576, 1024], P('seq'), may hold values from -6 to 6
- w_query: bfloat16 [1024, 512], P(None, 'head'), may hold values from -0.1875 to 0.1875
- w_key: bfloat16 [1024, 512], P(None, 'head'), may hold values from -0.1875 to 0.1875
- w_value: bfloat16 [1024, 512], P(None, 'head'), may hold values from -0.1875 to 0.1875
- w_out: bfloat16 [512, 1024], P('head'), may hold values from -0.25 to 0.25
- temper: float32 [4], replicated, may hold values from 3 to 6
Outputs:
- layer_out: bfloat16 [24576, 1024], P(('seq', 'head'))
The draws below stay inside these ranges and needn't reach their ends.
All inputs are finite; a program needn't handle non-finite values.
Results may differ from the reference program's by a relative error of at most 0.015.
Values may be sent and summed in bfloat16 or wider, within the bound.
A program may use at most 128 MiB of HBM per device.

```python
import math
import jax
import jax.numpy as jnp
from jax import lax

D = 1024
HEADS = 4
HD = 128
TOKENS = 24576


def steps_of(key, shape, split, low, high):
    def one(axis_at, blocks):
        heights = jax.random.uniform(jax.random.fold_in(jax.random.fold_in(key, 6), axis_at), (blocks,), jnp.float32, low / len(split), high / len(split))
        return jnp.repeat(jnp.exp(heights), shape[axis_at] // blocks).reshape((-1,) + (1,) * (len(shape) - axis_at - 1))

    factor_of = one(*split[0])
    for cut in split[1:]:
        factor_of = factor_of * one(*cut)
    return factor_of


def scatter_about(key, dims, scale, most, split=(), dtype=jnp.bfloat16):
    gain = steps_of(key, dims, split, -0.22, 0.18) if split else 1.0
    drawn = jax.random.normal(key, dims, jnp.float32) * scale * gain
    return jnp.minimum(jnp.maximum(drawn, -most), most).astype(dtype)


def setup_inputs(seed: int = 0) -> dict:
    key_list = jax.random.split(jax.random.key(seed), 7)
    tokens = scatter_about(key_list[0], (TOKENS, D), 1.0, 6.0, ((0, 128),))
    w_query = scatter_about(key_list[1], (D, HEADS * HD), D ** -0.5, 0.1875, ((1, 4),))
    w_key = scatter_about(key_list[2], (D, HEADS * HD), D ** -0.5, 0.1875, ((1, 4),))
    w_value = scatter_about(key_list[3], (D, HEADS * HD), D ** -0.5, 0.1875, ((1, 4),))
    w_out = scatter_about(key_list[4], (HEADS * HD, D), (HEADS * HD) ** -0.5, 0.25, ((0, 4),))
    temper = jnp.clip(jnp.exp(jax.random.uniform(key_list[5], (HEADS,), jnp.float32, math.log(3.0), math.log(6.0))), 3.0, 6.0)
    return dict(tokens=tokens, w_query=w_query, w_key=w_key, w_value=w_value, w_out=w_out, temper=temper)


EPS = 1e-06

def unit_heads(raw):
    return raw * lax.rsqrt(lax.optimization_barrier(jnp.mean(raw * raw, axis=-1, keepdims=True)) + EPS)

def reference(tokens, w_query, w_key, w_value, w_out, temper):
    query_raw = jnp.dot(tokens, w_query, preferred_element_type=jnp.float32).reshape(TOKENS, HEADS, HD)
    key_raw = jnp.dot(tokens, w_key, preferred_element_type=jnp.float32).reshape(TOKENS, HEADS, HD)
    value_raw = jnp.dot(tokens, w_value, preferred_element_type=jnp.float32).reshape(TOKENS, HEADS, HD)
    query_unit = unit_heads(query_raw).astype(jnp.bfloat16)
    key_unit = unit_heads(key_raw).astype(jnp.bfloat16).astype(jnp.float32)
    values = value_raw.astype(jnp.bfloat16).astype(jnp.float32)
    scale = temper / math.sqrt(HD)
    qblock = math.gcd(TOKENS, 512)

    def attend(query_block):
        score = jnp.einsum('qhd,khd->hqk', query_block.astype(jnp.float32), key_unit) * scale[:, None, None]
        weight = jnp.exp(score)
        total = lax.optimization_barrier(jnp.sum(weight, axis=-1))
        weight_b = weight.astype(jnp.bfloat16).astype(jnp.float32)
        summed = jnp.einsum('hqk,khd->qhd', weight_b, values)
        return (summed / jnp.transpose(total)[:, :, None]).astype(jnp.bfloat16)
    attended = lax.map(attend, query_unit.reshape(TOKENS // qblock, qblock, HEADS, HD))
    attended = attended.reshape(TOKENS, HEADS * HD)
    return jnp.dot(attended, w_out, preferred_element_type=jnp.float32).astype(jnp.bfloat16)
```

```python
import functools
import math

import jax
import jax.numpy as jnp
from jax import lax
from jax.experimental import pallas as pl
from jax.experimental.pallas import tpu as pltpu
from jax.sharding import PartitionSpec as P

MESH = pl.DeviceIdType.MESH
HD = 128
EPS = 1e-06
ROWS = 192
PART = 48
NZ = 8
F32 = jnp.float32
BF16 = jnp.bfloat16


def unit_rows(raw):
    return (raw * lax.rsqrt(jnp.mean(raw * raw, axis=-1, keepdims=True) + EPS)).astype(BF16)


class Gather:
    ORDER = (0, -1, 1, 2)

    def __init__(self, own, view, place, x_first, number, sems, first_target, target):
        self.own, self.view, self.place, self.x_first, self.number = own, view, place, x_first, number
        self.d_recv, self.send_sem, self.recv_sem = sems
        self.first_target, self.target = first_target, target
        self.table = []
        for i in self.ORDER:
            self.table += [(i, 0, None, 1), (i, 0, None, -1), (i, -1, 0, 1), (i, 1, 1, -1)]

    def at(self, i, j):
        x, y = self.place
        dx, dy = (i, j) if self.x_first else (j, i)
        return lax.rem(x + dx + 8, 4), lax.rem(y + dy + 8, 4)

    def first(self, n, received=False):
        at = self.at(-n, 0) if received else self.place
        return pltpu.make_async_remote_copy(
            src_ref=self.own,
            dst_ref=self.view(*at, None),
            send_sem=self.send_sem.at[self.number],
            recv_sem=self.d_recv.at[self.number * 4 + n],
            device_id=self.first_target(*self.at(n, 0)),
            device_id_type=MESH,
        )

    def copy(self, k, received):
        i, j, part, step = self.table[k]
        ref = self.view(*self.at(i, j - step if received else j), part)
        return self.along(k, ref, self.at(0, step))

    def along(self, k, ref, to):
        return pltpu.make_async_remote_copy(
            src_ref=ref,
            dst_ref=ref,
            send_sem=self.send_sem.at[self.number],
            recv_sem=self.recv_sem.at[self.number * 16 + k],
            device_id=self.target(*to),
            device_id_type=MESH,
        )

    def first_got(self, i):
        self.first((-i) % 4, True).wait_recv()

    def start(self, *ks):
        for k in ks:
            self.copy(k, False).start()

    def got(self, *ks):
        for k in ks:
            self.copy(k, True).wait_recv()

    def sent(self, ref):
        self.along(0, ref, self.at(0, 1)).wait_send()


def kernel(
    tok_hbm, wq_hbm, wk_hbm, wv_hbm, wo_hbm, temper_hbm, out_ref,
    temper, tok, wq, wk, wv, wall, qst, kst, vst, qbuf, kbuf, vbuf, acc,
    xo, xt, go, gt, so, st, ro, rt,
    load_sem, d_recv, g_send, g_recv, m_send, m_recv, w_send, w_recv, x_send, x_recv,
    q_send, q_recv, f_send, f_recv, o_send, o_recv, t_send, t_recv,
):
    s, h = lax.axis_index("seq"), lax.axis_index("head")
    x, y, zl = lax.div(s, 32), lax.rem(lax.div(s, 8), 4), lax.rem(s, 8)
    zh, c = lax.div(h, 2), lax.rem(h, 2)
    p = lax.rem(zl, 2)
    near = lax.div(zl, 4)
    other = h + 1 - 2 * c
    across = lax.rem(h + 2, 4)
    column = s - zl
    mine = c == p
    z_first = jnp.where(mine, zl, zl + 1 - 2 * p)
    h_first = jnp.where(mine, h, other)

    def rdma(src, dst, send, recv, dev):
        return pltpu.make_async_remote_copy(
            src_ref=src, dst_ref=dst, send_sem=send, recv_sem=recv, device_id=dev, device_id_type=MESH
        )

    loads = [
        pltpu.make_async_copy(src, dst, load_sem.at[i])
        for i, (src, dst) in enumerate(
            [
                (tok_hbm, tok),
                (wk_hbm, wk),
                (wv_hbm, wv),
                (wq_hbm, wq),
                (wo_hbm, wall.at[pl.ds(pl.multiple_of(h * HD, HD), HD)]),
                (temper_hbm, temper),
            ]
        )
    ]
    for load in loads:
        load.start()

    barrier = pltpu.get_barrier_semaphore()

    def plane(px, py):
        return ((px * 4 + py) * 8 + zl, h)

    def first_plane(px, py):
        return ((px * 4 + py) * 8 + z_first, h_first)

    def greet_plane(where):
        for n in (1, 2, 3):
            for at in ((lax.rem(x + n, 4), y), (x, lax.rem(y + n, 4))):
                pl.semaphore_signal(barrier, inc=1, device_id=where(*at), device_id_type=MESH)

    greet_plane(plane)

    @pl.when(jnp.logical_not(mine))
    def _():
        greet_plane(first_plane)

    def greet(o, carry):
        at = lax.rem(zl * 4 + h + o, 32)
        pl.semaphore_signal(
            barrier, inc=1, device_id=(column + lax.div(at, 4), lax.rem(at, 4)), device_id_type=MESH
        )
        return carry

    lax.fori_loop(1, 32, greet, 0)
    acc[...] = jnp.zeros_like(acc)

    def rows_of(px, py, part):
        first = (py * 4 + px) * ROWS
        if part is None:
            return pl.ds(pl.multiple_of(first, ROWS), ROWS)
        return pl.ds(pl.multiple_of(first + part * (ROWS // 2), ROWS // 2), ROWS // 2)

    def k_view(px, py, part):
        return kbuf.at[rows_of(px, py, part)]

    def v_view(px, py, part):
        return vbuf.at[rows_of(px, py, part)]

    sems = (d_recv, g_send, g_recv)
    keys = Gather(kst, k_view, (x, y), True, 0, sems, first_plane, plane)
    vals = Gather(vst, v_view, (x, y), False, 1, sems, first_plane, plane)

    def head_rows(head):
        return wall.at[pl.ds(pl.multiple_of(head * HD, HD), HD)]

    def w_piece(head, px):
        first = pl.multiple_of(head * HD + lax.rem(px, 2) * 64, 64)
        lanes = pl.multiple_of((y * 2 + lax.div(px, 2)) * 128, 128)
        return wall.at[pl.ds(first, 64), pl.ds(lanes, 128)]

    def w_row(head, py):
        return wall.at[pl.ds(pl.multiple_of(head * HD, HD), HD), pl.ds(pl.multiple_of(py * 256, 256), 256)]

    def w_share_x(n, received=False):
        ref = w_piece(across, lax.rem(x + 4 - n, 4) if received else x)
        return rdma(ref, ref, w_send.at[0], w_recv.at[n], plane(lax.rem(x + n, 4), y))

    def w_share_y(n, received=False):
        ref = w_row(across, lax.rem(y + 4 - n, 4) if received else y)
        return rdma(ref, ref, w_send.at[1], w_recv.at[4 + n], plane(x, lax.rem(y + n, 4)))

    w_across = rdma(w_piece(h, x), w_piece(h, x), m_send.at[0], m_recv.at[0], (s, across))
    w_across_in = rdma(w_piece(across, x), w_piece(across, x), m_send.at[0], m_recv.at[0], (s, across))
    w_other = rdma(head_rows(h), head_rows(h), m_send.at[1], m_recv.at[1], (s, other))
    w_other_in = rdma(head_rows(other), head_rows(other), m_send.at[1], m_recv.at[1], (s, other))
    far_other = lax.rem(other + 2, 4)
    w_last = rdma(head_rows(across), head_rows(across), m_send.at[2], m_recv.at[2], (s, other))
    w_last_in = rdma(head_rows(far_other), head_rows(far_other), m_send.at[2], m_recv.at[2], (s, other))

    loads[0].wait()
    loads[1].wait()
    key_unit = unit_rows(jnp.dot(tok[...], wk[...], preferred_element_type=F32))
    kst[...] = key_unit

    @pl.when(mine)
    def _():
        kbuf[rows_of(x, y, None)] = key_unit
        pl.semaphore_wait(barrier, 37)

    @pl.when(jnp.logical_not(mine))
    def _():
        pl.semaphore_wait(barrier, 43)

    def give_first(g):
        for n in (1, 3, 2):
            g.first(n).start()

        @pl.when(jnp.logical_not(mine))
        def _():
            g.first(0).start()

        @pl.when(mine)
        def _():
            g.start(0, 1)

    give_first(keys)
    loads[4].wait()
    w_across.start()
    w_other.start()
    loads[2].wait()
    value = jnp.dot(tok[...], wv[...], preferred_element_type=F32).astype(BF16)
    vst[...] = value

    @pl.when(mine)
    def _():
        vbuf[rows_of(x, y, None)] = value

    give_first(vals)

    loads[3].wait()
    query_unit = unit_rows(jnp.dot(tok[...], wq[...], preferred_element_type=F32))
    qst[...] = query_unit

    def q_view(u):
        return qbuf.at[pl.ds(pl.multiple_of(u * ROWS, ROWS), ROWS)]

    half, bit = lax.div(zl, 4), lax.rem(lax.div(zl, 2), 2)
    q_targets = (half * 2 + bit, half * 2 + 1 - bit, 2 - half * 2 + bit, 3 - half * 2 - bit)
    q_self = jnp.logical_and(mine, near == c)

    def q_copy(n):
        return rdma(
            qst,
            q_view(zl),
            q_send.at[n],
            q_recv.at[lax.rem(zl, 4)],
            (column + c + 2 * q_targets[n], zh * 2 + near),
        )

    @pl.when(q_self)
    def _():
        qbuf[pl.ds(pl.multiple_of(zl * ROWS, ROWS), ROWS)] = query_unit

    @pl.when(jnp.logical_not(q_self))
    def _():
        q_copy(0).start()

    q_copy(1).start()
    loads[5].wait()

    @pl.when(jnp.logical_not(mine))
    def _():
        for g in (keys, vals):
            g.first_got(0)
            g.start(0, 1)

    for t, i in ((1, -1), (2, 1), (3, 2)):
        for g in (keys, vals):
            g.first_got(i)
            g.start(4 * t, 4 * t + 1)

    for n in (2, 3):
        q_copy(n).start()

    def relay(g, t):
        g.got(4 * t)
        g.start(4 * t + 2)
        g.got(4 * t + 1)
        g.start(4 * t + 3)

    for t in (0, 1, 2):
        for g in (keys, vals):
            relay(g, t)
    w_across_in.wait_recv()
    for n in (1, 3, 2):
        w_share_x(n).start()
    vals.got(2, 3)

    def unit_at(k):
        return k + near * (7 - 2 * k)

    def q_arrived(k):
        u = unit_at(k)
        slot = lax.rem(u, 4)
        first_core = (near == c) if k < 4 else (near != c)
        forward = rdma(q_view(u), q_view(u), f_send.at[slot], f_recv.at[slot], (s, other))
        direct = rdma(q_view(u), q_view(u), q_send.at[0], q_recv.at[slot], (s, other))

        @pl.when(first_core)
        def _():
            if k < 4:

                @pl.when(jnp.logical_not(jnp.logical_and(q_self, u == zl)))
                def _():
                    direct.wait_recv()
            else:
                direct.wait_recv()
            forward.start()

        @pl.when(jnp.logical_not(first_core))
        def _():
            forward.wait_recv()

    scale = temper[zh * 2 + p] * F32(math.log2(math.e) / math.sqrt(HD))

    ones = jnp.ones((4 * ROWS, HD), BF16)

    def piece(half, dy):
        q0 = pl.multiple_of(half * (4 * ROWS), 4 * ROWS)
        k0 = pl.multiple_of(lax.rem(y + dy, 4) * (4 * ROWS), 4 * ROWS)
        score = lax.dot_general(
            qbuf[pl.ds(q0, 4 * ROWS)],
            kbuf[pl.ds(k0, 4 * ROWS)],
            (((1,), (1,)), ((), ())),
            preferred_element_type=F32,
        )
        weight = jnp.exp2(score * scale).astype(BF16)
        value_block = jnp.concatenate([vbuf[pl.ds(k0, 4 * ROWS)], ones], axis=1)
        acc[pl.ds(q0, 4 * ROWS)] += jnp.dot(weight, value_block, preferred_element_type=F32)

    lane = lax.broadcasted_iota(jnp.int32, (PART, HD), 1)
    row = lax.broadcasted_iota(jnp.int32, (PART, HD), 0)
    diagonal = lane == row
    slot = (zh * 2 + p) * 4 + lax.div(zl, 2)

    def part_rows(core, i):
        return pl.ds(pl.multiple_of(core * (4 * ROWS) + i * PART, PART), PART)

    def give_copies(n):
        at = pl.ds(n * 4, 4)
        return (
            rdma(xo.at[at], go.at[at], x_send.at[0], x_recv.at[n], (s, other)),
            rdma(xt.at[at], gt.at[at], x_send.at[1], x_recv.at[4 + n], (s, other)),
        )

    def block_of(core, i):
        block = acc[part_rows(core, i)]
        return block[:, :HD], jnp.sum(jnp.where(diagonal, block[:, HD:], 0.0), axis=0, keepdims=True)

    def give(n, carry):
        def one(k, inner):
            i = n * 4 + k
            summed, xt[i] = block_of(1 - c, i)
            xo[i] = summed.astype(BF16)
            return inner

        lax.fori_loop(0, 4, one, 0)
        for copy in give_copies(n):
            copy.start()
        return carry

    def o_copy(i):
        dev = (column + c * 4 + lax.div(i, 4), lax.rem(i, 4))
        return (
            rdma(so.at[i], ro.at[slot], o_send, o_recv, dev),
            rdma(st.at[i], rt.at[slot], t_send, t_recv, dev),
        )

    def o_self(i):
        return jnp.logical_and(c * 4 + lax.div(i, 4) == zl, lax.rem(i, 4) == h)

    def settle(n, carry):
        for copy in give_copies(n):
            copy.wait_recv()

        def one(k, inner):
            i = n * 4 + k
            summed, total = block_of(c, i)
            summed, total = (summed + go[i].astype(F32)).astype(BF16), total + gt[i]
            so[i], st[i] = summed, total

            @pl.when(o_self(i))
            def _():
                ro[slot], rt[slot] = summed, total

            @pl.when(jnp.logical_not(o_self(i)))
            def _():
                for copy in o_copy(i):
                    copy.start()

            return inner

        lax.fori_loop(0, 4, one, 0)
        return carry

    def step(i, carry):
        def at(n, events):
            @pl.when(i == n)
            def _():
                events()

        def before_1():
            for g in (keys, vals):
                relay(g, 3)
            vals.got(6, 7)
            for n in (1, 3, 2):
                w_share_x(n, True).wait_recv()
            for n in (1, 3, 2):
                w_share_y(n).start()

        def before_2():
            vals.got(10, 11)

        def before_3():
            for k in range(4, 8):
                q_arrived(k)
            for n in (1, 3, 2):
                w_share_y(n, True).wait_recv()
            w_last.start()

        def before_6():
            keys.got(2, 3, 6, 7, 10, 11, 14, 15)
            vals.got(14, 15)

        def before_7():
            @pl.when(near != c)
            def _():
                lax.fori_loop(0, 4, give, 0)

        at(1, before_1)
        at(2, before_2)
        at(3, before_3)
        at(6, before_6)
        at(7, before_7)
        near_now = jnp.logical_or(i < 3, i == 6)
        r = jnp.where(i >= 6, 3, lax.rem(i, 3))
        piece(
            jnp.where(near_now, near, 1 - near),
            jnp.where(r == 0, 0, jnp.where(r == 1, 3, jnp.where(r == 2, 1, 2))),
        )
        return carry

    for k in range(4):
        q_arrived(k)
    lax.fori_loop(0, 8, step, 0)

    @pl.when(near == c)
    def _():
        lax.fori_loop(0, 4, give, 0)

    lax.fori_loop(0, 4, settle, 0)

    for g, ref in ((keys, kbuf), (vals, vbuf)):
        @pl.when(mine)
        def _():
            g.sent(ref.at[pl.ds(0, 15 * ROWS)])

        @pl.when(jnp.logical_not(mine))
        def _():
            g.sent(ref)

    for copy in (w_across, w_other, w_last):
        copy.wait_send()
    three_pieces = wall.at[pl.ds(0, 64), pl.ds(0, 384)]
    three_rows = wall.at[pl.ds(0, HD), pl.ds(0, 768)]
    rdma(three_pieces, three_pieces, w_send.at[0], w_recv.at[1], plane(lax.rem(x + 1, 4), y)).wait_send()
    rdma(three_rows, three_rows, w_send.at[1], w_recv.at[5], plane(x, lax.rem(y + 1, 4))).wait_send()
    rdma(xo, go, x_send.at[0], x_recv.at[0], (s, other)).wait_send()
    rdma(xt, gt, x_send.at[1], x_recv.at[4], (s, other)).wait_send()

    @pl.when(jnp.logical_not(q_self))
    def _():
        q_copy(0).wait_send()

    for n in (1, 2, 3):
        q_copy(n).wait_send()

    def forwarded(i, carry):
        rdma(q_view(c * 4 + i), q_view(c * 4 + i), f_send.at[i], f_recv.at[i], (s, other)).wait_send()
        return carry

    lax.fori_loop(0, 4, forwarded, 0)

    w_other_in.wait_recv()
    w_last_in.wait_recv()

    def all_parts(count):
        at = pl.ds(0, count)
        return (
            rdma(so.at[at], ro.at[at], o_send, o_recv, (s, other)),
            rdma(st.at[at], rt.at[at], t_send, t_recv, (s, other)),
        )

    @pl.when(near == c)
    def _():
        for copy in all_parts(15):
            copy.wait_recv()

    @pl.when(near != c)
    def _():
        for copy in all_parts(16):
            copy.wait_recv()

    attended = []
    for head in range(4):
        summed = sum(ro[head * 4 + j].astype(F32) for j in range(4))
        total = sum(rt[head * 4 + j] for j in range(4))
        total = jnp.sum(jnp.where(diagonal, jnp.broadcast_to(total, (PART, HD)), 0.0), axis=1, keepdims=True)
        attended.append((summed / total).astype(BF16))
    out_ref[...] = jnp.dot(
        jnp.concatenate(attended, axis=1), wall[...], preferred_element_type=F32
    ).astype(BF16)

    @pl.when(near == c)
    def _():
        for copy in all_parts(15):
            copy.wait_send()

    @pl.when(near != c)
    def _():
        for copy in all_parts(16):
            copy.wait_send()


def on_device(tokens, w_query, w_key, w_value, w_out, temper):
    dma = pltpu.SemaphoreType.DMA
    d_model = tokens.shape[1]
    return pl.pallas_call(
        kernel,
        out_shape=jax.ShapeDtypeStruct((PART, d_model), BF16),
        in_specs=[pl.BlockSpec(memory_space=pltpu.HBM)] * 6,
        out_specs=pl.BlockSpec(memory_space=pltpu.VMEM),
        scratch_shapes=[
            pltpu.SMEM((4,), F32),
            pltpu.VMEM((ROWS, d_model), BF16),
            pltpu.VMEM((d_model, HD), BF16),
            pltpu.VMEM((d_model, HD), BF16),
            pltpu.VMEM((d_model, HD), BF16),
            pltpu.VMEM((4 * HD, d_model), BF16),
            pltpu.VMEM((ROWS, HD), BF16),
            pltpu.VMEM((ROWS, HD), BF16),
            pltpu.VMEM((ROWS, HD), BF16),
            pltpu.VMEM((NZ * ROWS, HD), BF16),
            pltpu.VMEM((16 * ROWS, HD), BF16),
            pltpu.VMEM((16 * ROWS, HD), BF16),
            pltpu.VMEM((NZ * ROWS, 2 * HD), F32),
            pltpu.VMEM((16, PART, HD), BF16),
            pltpu.VMEM((16, 1, HD), F32),
            pltpu.VMEM((16, PART, HD), BF16),
            pltpu.VMEM((16, 1, HD), F32),
            pltpu.VMEM((16, PART, HD), BF16),
            pltpu.VMEM((16, 1, HD), F32),
            pltpu.VMEM((16, PART, HD), BF16),
            pltpu.VMEM((16, 1, HD), F32),
            dma((6,)),
            dma((8,)),
            dma((2,)),
            dma((32,)),
            dma((3,)),
            dma((3,)),
            dma((2,)),
            dma((8,)),
            dma((2,)),
            dma((8,)),
            dma((4,)),
            dma((4,)),
            dma((4,)),
            dma((4,)),
            dma(()),
            dma(()),
            dma(()),
            dma(()),
        ],
        compiler_params=pltpu.CompilerParams(
            collective_id=0, has_side_effects=True, vmem_limit_bytes=58 * 1024 * 1024
        ),
        name="layer",
    )(tokens, w_query, w_key, w_value, w_out, temper)


def solution(mesh):
    return jax.shard_map(
        on_device,
        mesh=mesh,
        in_specs=(
            P("seq", None),
            P(None, "head"),
            P(None, "head"),
            P(None, "head"),
            P("head", None),
            P(),
        ),
        out_specs=P(("seq", "head"), None),
        check_vma=False,
    )
```

```python
import functools
import math

import jax
import jax.numpy as jnp
from jax import lax
from jax.experimental import pallas as pl
from jax.experimental.pallas import tpu as pltpu
from jax.sharding import PartitionSpec as P

MESH = pl.DeviceIdType.MESH
HD = 128
EPS = 1e-06
ROWS = 192
PART = 48
NZ = 8
F32 = jnp.float32
BF16 = jnp.bfloat16


def unit_rows(raw):
    return (raw * lax.rsqrt(jnp.mean(raw * raw, axis=-1, keepdims=True) + EPS)).astype(BF16)


class Gather:
    ORDER = (0, -1, 1, 2)

    def __init__(self, own, view, place, x_first, number, sems, first_target, target):
        self.own, self.view, self.place, self.x_first, self.number = own, view, place, x_first, number
        self.d_recv, self.send_sem, self.recv_sem = sems
        self.first_target, self.target = first_target, target
        self.table = []
        for i in self.ORDER:
            self.table += [(i, 0, None, 1), (i, 0, None, -1), (i, -1, 0, 1), (i, 1, 1, -1)]

    def at(self, i, j):
        x, y = self.place
        dx, dy = (i, j) if self.x_first else (j, i)
        return lax.rem(x + dx + 8, 4), lax.rem(y + dy + 8, 4)

    def first(self, n, received=False):
        at = self.at(-n, 0) if received else self.place
        return pltpu.make_async_remote_copy(
            src_ref=self.own,
            dst_ref=self.view(*at, None),
            send_sem=self.send_sem.at[self.number],
            recv_sem=self.d_recv.at[self.number * 4 + n],
            device_id=self.first_target(*self.at(n, 0)),
            device_id_type=MESH,
        )

    def copy(self, k, received):
        i, j, part, step = self.table[k]
        ref = self.view(*self.at(i, j - step if received else j), part)
        return self.along(k, ref, self.at(0, step))

    def along(self, k, ref, to):
        return pltpu.make_async_remote_copy(
            src_ref=ref,
            dst_ref=ref,
            send_sem=self.send_sem.at[self.number],
            recv_sem=self.recv_sem.at[self.number * 16 + k],
            device_id=self.target(*to),
            device_id_type=MESH,
        )

    def first_got(self, i):
        self.first((-i) % 4, True).wait_recv()

    def start(self, *ks):
        for k in ks:
            self.copy(k, False).start()

    def got(self, *ks):
        for k in ks:
            self.copy(k, True).wait_recv()

    def sent(self, ref):
        self.along(0, ref, self.at(0, 1)).wait_send()


def kernel(
    tok_hbm, wq_hbm, wk_hbm, wv_hbm, wo_hbm, temper_hbm, out_ref,
    temper, tok, wq, wkv, wall, qst, kvst, qbuf, kv_a, kv_b, acc,
    xo, xt, go, gt, so, st, ro, rt,
    load_sem, d_recv, g_send, g_recv, m_send, m_recv, w_send, w_recv, x_send, x_recv,
    q_send, q_recv, f_send, f_recv, o_send, o_recv, t_send, t_recv, ready,
):
    s, h = lax.axis_index("seq"), lax.axis_index("head")
    x, y, zl = lax.div(s, 32), lax.rem(lax.div(s, 8), 4), lax.rem(s, 8)
    zh, c = lax.div(h, 2), lax.rem(h, 2)
    p = lax.rem(zl, 2)
    near = lax.div(zl, 4)
    other = h + 1 - 2 * c
    across = lax.rem(h + 2, 4)
    column = s - zl
    mine = c == p
    z_first = jnp.where(mine, zl, zl + 1 - 2 * p)
    h_first = jnp.where(mine, h, other)

    def rdma(src, dst, send, recv, dev):
        return pltpu.make_async_remote_copy(
            src_ref=src, dst_ref=dst, send_sem=send, recv_sem=recv, device_id=dev, device_id_type=MESH
        )

    barrier = pltpu.get_barrier_semaphore()

    def plane(px, py):
        return ((px * 4 + py) * 8 + zl, h)

    def first_plane(px, py):
        return ((px * 4 + py) * 8 + z_first, h_first)

    def greet(dev):
        pl.semaphore_signal(barrier, inc=1, device_id=dev, device_id_type=MESH)

    def greet_plane(where):
        for n in (1, 3, 2):
            greet(where(lax.rem(x + n, 4), y))
            greet(where(x, lax.rem(y + n, 4)))

    q_self = jnp.logical_and(mine, near == c)

    @pl.when(jnp.logical_not(mine))
    def _():
        greet_plane(first_plane)
        greet(first_plane(x, y))

    greet_plane(plane)
    greet((s, other))
    greet((s, across))
    for n in range(4):

        @pl.when(jnp.logical_not(jnp.logical_and(q_self, c * 4 + n == zl)))
        def _():
            greet((column + c * 4 + n, zh * 2 + p))

    loads = [
        pltpu.make_async_copy(src, dst, load_sem.at[i])
        for i, (src, dst) in enumerate(
            [
                (tok_hbm, tok),
                (wk_hbm, wkv.at[:, pl.ds(0, HD)]),
                (wv_hbm, wkv.at[:, pl.ds(HD, HD)]),
                (wq_hbm, wq),
                (wo_hbm, wall.at[pl.ds(pl.multiple_of(h * HD, HD), HD)]),
                (temper_hbm, temper),
            ]
        )
    ]
    for load in loads:
        load.start()

    acc[...] = jnp.zeros_like(acc)

    half_rows = ROWS // 2

    def rows_of(at, part):
        if part is None:
            return pl.ds(pl.multiple_of(at * half_rows, half_rows), half_rows)
        return pl.ds(pl.multiple_of(at * half_rows + part * PART, PART), PART)

    def a_view(px, py, part):
        return kv_a.at[rows_of(py * 4 + px, part)]

    def b_view(px, py, part):
        return kv_b.at[rows_of(px * 4 + py, part)]

    sems = (d_recv, g_send, g_recv)
    along_x = Gather(kvst.at[pl.ds(0, half_rows)], a_view, (x, y), True, 0, sems, first_plane, plane)
    along_y = Gather(kvst.at[pl.ds(half_rows, half_rows)], b_view, (x, y), False, 1, sems, first_plane, plane)
    gathers = (along_x, along_y)

    def head_rows(head):
        return wall.at[pl.ds(pl.multiple_of(head * HD, HD), HD)]

    def w_piece(head, px):
        first = pl.multiple_of(head * HD + lax.rem(px, 2) * 64, 64)
        lanes = pl.multiple_of((y * 2 + lax.div(px, 2)) * 128, 128)
        return wall.at[pl.ds(first, 64), pl.ds(lanes, 128)]

    def w_row(head, py):
        return wall.at[pl.ds(pl.multiple_of(head * HD, HD), HD), pl.ds(pl.multiple_of(py * 256, 256), 256)]

    def w_share_x(n, received=False):
        ref = w_piece(across, lax.rem(x + 4 - n, 4) if received else x)
        return rdma(ref, ref, w_send.at[0], w_recv.at[n], plane(lax.rem(x + n, 4), y))

    def w_share_y(n, received=False):
        ref = w_row(across, lax.rem(y + 4 - n, 4) if received else y)
        return rdma(ref, ref, w_send.at[1], w_recv.at[4 + n], plane(x, lax.rem(y + n, 4)))

    w_across = rdma(w_piece(h, x), w_piece(h, x), m_send.at[0], m_recv.at[0], (s, across))
    w_across_in = rdma(w_piece(across, x), w_piece(across, x), m_send.at[0], m_recv.at[0], (s, across))
    w_other = rdma(head_rows(h), head_rows(h), m_send.at[1], m_recv.at[1], (s, other))
    w_other_in = rdma(head_rows(other), head_rows(other), m_send.at[1], m_recv.at[1], (s, other))
    far_other = lax.rem(other + 2, 4)
    w_last = rdma(head_rows(across), head_rows(across), m_send.at[2], m_recv.at[2], (s, other))
    w_last_in = rdma(head_rows(far_other), head_rows(far_other), m_send.at[2], m_recv.at[2], (s, other))

    loads[0].wait()
    loads[1].wait()
    loads[2].wait()
    raw = jnp.dot(tok[...], wkv[...], preferred_element_type=F32)
    both = jnp.concatenate([unit_rows(raw[:, :HD]), raw[:, HD:].astype(BF16)], axis=1)
    kvst[...] = both

    @pl.when(mine)
    def _():
        kv_a[rows_of(y * 4 + x, None)] = both[:half_rows]
        kv_b[rows_of(x * 4 + y, None)] = both[half_rows:]
        pl.semaphore_wait(barrier, 12 - jnp.where(near == c, 1, 0))

    @pl.when(jnp.logical_not(mine))
    def _():
        pl.semaphore_wait(barrier, 19)

    def give_first(g):
        for n in (1, 3, 2):
            g.first(n).start()

        @pl.when(jnp.logical_not(mine))
        def _():
            g.first(0).start()

        @pl.when(mine)
        def _():
            g.start(0, 1)

    give_first(along_x)
    give_first(along_y)
    loads[4].wait()
    w_across.start()
    loads[3].wait()
    query_unit = unit_rows(jnp.dot(tok[...], wq[...], preferred_element_type=F32))
    qst[...] = query_unit

    def q_view(u):
        return qbuf.at[pl.ds(pl.multiple_of(u * ROWS, ROWS), ROWS)]

    half, bit = lax.div(zl, 4), lax.rem(lax.div(zl, 2), 2)
    q_targets = (half * 2 + bit, half * 2 + 1 - bit, 2 - half * 2 + bit, 3 - half * 2 - bit)

    def q_copy(n):
        return rdma(
            qst,
            q_view(zl),
            q_send.at[n],
            q_recv.at[lax.rem(zl, 4)],
            (column + c + 2 * q_targets[n], zh * 2 + near),
        )

    @pl.when(q_self)
    def _():
        qbuf[pl.ds(pl.multiple_of(zl * ROWS, ROWS), ROWS)] = query_unit

    @pl.when(jnp.logical_not(q_self))
    def _():
        q_copy(0).start()

    q_copy(1).start()
    loads[5].wait()
    w_other.start()

    @pl.when(jnp.logical_not(mine))
    def _():
        for g in gathers:
            g.first_got(0)
            g.start(0, 1)

    for t, i in ((1, -1), (2, 1), (3, 2)):
        for g in gathers:
            g.first_got(i)
            g.start(4 * t, 4 * t + 1)

    for n in (2, 3):
        q_copy(n).start()

    def relay(g, t):
        g.got(4 * t)
        g.start(4 * t + 2)
        g.got(4 * t + 1)
        g.start(4 * t + 3)

    def unit_at(k):
        return k + near * (7 - 2 * k)

    def q_arrived(k):
        u = unit_at(k)
        slot = lax.rem(u, 4)
        first_core = (near == c) if k < 4 else (near != c)
        forward = rdma(q_view(u), q_view(u), f_send.at[slot], f_recv.at[slot], (s, other))
        direct = rdma(q_view(u), q_view(u), q_send.at[0], q_recv.at[slot], (s, other))

        @pl.when(first_core)
        def _():
            if k < 4:

                @pl.when(jnp.logical_not(jnp.logical_and(q_self, u == zl)))
                def _():
                    direct.wait_recv()
            else:
                direct.wait_recv()
            forward.start()

        @pl.when(jnp.logical_not(first_core))
        def _():
            forward.wait_recv()

    scale = temper[zh * 2 + p] * F32(math.log2(math.e) / math.sqrt(HD))

    ones = jnp.ones((4 * ROWS, HD), BF16)

    def piece(half, d):
        q0 = pl.multiple_of(half * (4 * ROWS), 4 * ROWS)
        a0 = pl.multiple_of(lax.rem(y + d, 4) * (2 * ROWS), 2 * ROWS)
        b0 = pl.multiple_of(lax.rem(x + d, 4) * (2 * ROWS), 2 * ROWS)
        both_k = jnp.concatenate([kv_a[pl.ds(a0, 2 * ROWS), :HD], kv_b[pl.ds(b0, 2 * ROWS), :HD]], axis=0)
        both_v = jnp.concatenate([kv_a[pl.ds(a0, 2 * ROWS), HD:], kv_b[pl.ds(b0, 2 * ROWS), HD:]], axis=0)
        score = lax.dot_general(
            qbuf[pl.ds(q0, 4 * ROWS)], both_k, (((1,), (1,)), ((), ())), preferred_element_type=F32
        )
        weight = jnp.exp2(score * scale).astype(BF16)
        value_block = jnp.concatenate([both_v, ones], axis=1)
        acc[pl.ds(q0, 4 * ROWS)] += jnp.dot(weight, value_block, preferred_element_type=F32)

    lane = lax.broadcasted_iota(jnp.int32, (PART, HD), 1)
    row = lax.broadcasted_iota(jnp.int32, (PART, HD), 0)
    diagonal = lane == row
    slot = (zh * 2 + p) * 4 + lax.div(zl, 2)

    def part_rows(core, i):
        return pl.ds(pl.multiple_of(core * (4 * ROWS) + i * PART, PART), PART)

    def give_copies(n):
        at = pl.ds(n * 4, 4)
        return (
            rdma(xo.at[at], go.at[at], x_send.at[0], x_recv.at[n], (s, other)),
            rdma(xt.at[at], gt.at[at], x_send.at[1], x_recv.at[4 + n], (s, other)),
        )

    def block_of(core, i):
        block = acc[part_rows(core, i)]
        return block[:, :HD], jnp.sum(jnp.where(diagonal, block[:, HD:], 0.0), axis=0, keepdims=True)

    def give(n, carry):
        def one(k, inner):
            i = n * 4 + k
            summed, xt[i] = block_of(1 - c, i)
            xo[i] = summed.astype(BF16)
            return inner

        lax.fori_loop(0, 4, one, 0)
        for copy in give_copies(n):
            copy.start()
        return carry

    def o_copy(i):
        dev = (column + c * 4 + lax.div(i, 4), lax.rem(i, 4))
        return (
            rdma(so.at[i], ro.at[slot], o_send, o_recv, dev),
            rdma(st.at[i], rt.at[slot], t_send, t_recv, dev),
        )

    def o_self(i):
        return jnp.logical_and(c * 4 + lax.div(i, 4) == zl, lax.rem(i, 4) == h)

    def settle(n, carry):
        for copy in give_copies(n):
            copy.wait_recv()

        def one(k, inner):
            i = n * 4 + k
            summed, total = block_of(c, i)
            summed, total = (summed + go[i].astype(F32)).astype(BF16), total + gt[i]
            so[i], st[i] = summed, total

            @pl.when(o_self(i))
            def _():
                ro[slot], rt[slot] = summed, total

            @pl.when(jnp.logical_not(o_self(i)))
            def _():
                for copy in o_copy(i):
                    copy.start()

            return inner

        lax.fori_loop(0, 4, one, 0)
        return carry

    def step(i, carry):
        def at(n, events):
            @pl.when(i == n)
            def _():
                events()

        def before_1():
            for t in range(4):
                for g in gathers:
                    relay(g, t)
            w_across_in.wait_recv()
            for n in (1, 3, 2):
                w_share_x(n).start()

        def before_3():
            for k in range(4, 8):
                q_arrived(k)
            pl.semaphore_signal(ready, inc=1, device_id=(s, across), device_id_type=MESH)
            for n in (1, 3, 2):
                w_share_x(n, True).wait_recv()
            for n in (1, 3, 2):
                w_share_y(n).start()

        def before_6():
            for g in gathers:
                g.got(2, 3, 6, 7, 10, 11, 14, 15)
            for n in (1, 3, 2):
                w_share_y(n, True).wait_recv()

        def before_7():
            @pl.when(near != c)
            def _():
                lax.fori_loop(0, 4, give, 0)

        at(1, before_1)
        at(3, before_3)
        at(6, before_6)
        at(7, before_7)
        near_now = jnp.logical_or(i < 3, i == 6)
        r = jnp.where(i >= 6, 3, lax.rem(i, 3))
        piece(
            jnp.where(near_now, near, 1 - near),
            jnp.where(r == 0, 0, jnp.where(r == 1, 3, jnp.where(r == 2, 1, 2))),
        )
        return carry

    for k in range(4):
        q_arrived(k)
    lax.fori_loop(0, 8, step, 0)

    @pl.when(near == c)
    def _():
        lax.fori_loop(0, 4, give, 0)

    w_last.start()
    pl.semaphore_wait(ready, 1)
    lax.fori_loop(0, 4, settle, 0)

    for g, ref in ((along_x, kv_a), (along_y, kv_b)):
        @pl.when(mine)
        def _():
            g.sent(ref.at[pl.ds(0, 15 * half_rows)])

        @pl.when(jnp.logical_not(mine))
        def _():
            g.sent(ref)

    for copy in (w_across, w_other, w_last):
        copy.wait_send()
    three_pieces = wall.at[pl.ds(0, 64), pl.ds(0, 384)]
    three_rows = wall.at[pl.ds(0, HD), pl.ds(0, 768)]
    rdma(three_pieces, three_pieces, w_send.at[0], w_recv.at[1], plane(lax.rem(x + 1, 4), y)).wait_send()
    rdma(three_rows, three_rows, w_send.at[1], w_recv.at[5], plane(x, lax.rem(y + 1, 4))).wait_send()
    rdma(xo, go, x_send.at[0], x_recv.at[0], (s, other)).wait_send()
    rdma(xt, gt, x_send.at[1], x_recv.at[4], (s, other)).wait_send()

    @pl.when(jnp.logical_not(q_self))
    def _():
        q_copy(0).wait_send()

    for n in (1, 2, 3):
        q_copy(n).wait_send()

    def forwarded(i, carry):
        rdma(q_view(c * 4 + i), q_view(c * 4 + i), f_send.at[i], f_recv.at[i], (s, other)).wait_send()
        return carry

    lax.fori_loop(0, 4, forwarded, 0)

    w_other_in.wait_recv()
    w_last_in.wait_recv()

    def all_parts(count):
        at = pl.ds(0, count)
        return (
            rdma(so.at[at], ro.at[at], o_send, o_recv, (s, other)),
            rdma(st.at[at], rt.at[at], t_send, t_recv, (s, other)),
        )

    @pl.when(near == c)
    def _():
        for copy in all_parts(15):
            copy.wait_recv()

    @pl.when(near != c)
    def _():
        for copy in all_parts(16):
            copy.wait_recv()

    attended = []
    for head in range(4):
        summed = sum(ro[head * 4 + j].astype(F32) for j in range(4))
        total = sum(rt[head * 4 + j] for j in range(4))
        total = jnp.sum(jnp.where(diagonal, jnp.broadcast_to(total, (PART, HD)), 0.0), axis=1, keepdims=True)
        attended.append((summed / total).astype(BF16))
    out_ref[...] = jnp.dot(
        jnp.concatenate(attended, axis=1), wall[...], preferred_element_type=F32
    ).astype(BF16)

    @pl.when(near == c)
    def _():
        for copy in all_parts(15):
            copy.wait_send()

    @pl.when(near != c)
    def _():
        for copy in all_parts(16):
            copy.wait_send()


def on_device(tokens, w_query, w_key, w_value, w_out, temper):
    dma = pltpu.SemaphoreType.DMA
    args = [
        pltpu.with_memory_space_constraint(a, pltpu.HBM)
        for a in (tokens, w_query, w_key, w_value, w_out, temper)
    ]
    d_model = tokens.shape[1]
    return pl.pallas_call(
        kernel,
        out_shape=jax.ShapeDtypeStruct((PART, d_model), BF16),
        in_specs=[pl.BlockSpec(memory_space=pltpu.HBM)] * 6,
        out_specs=pl.BlockSpec(memory_space=pltpu.VMEM),
        scratch_shapes=[
            pltpu.SMEM((4,), F32),
            pltpu.VMEM((ROWS, d_model), BF16),
            pltpu.VMEM((d_model, HD), BF16),
            pltpu.VMEM((d_model, 2 * HD), BF16),
            pltpu.VMEM((4 * HD, d_model), BF16),
            pltpu.VMEM((ROWS, HD), BF16),
            pltpu.VMEM((ROWS, 2 * HD), BF16),
            pltpu.VMEM((NZ * ROWS, HD), BF16),
            pltpu.VMEM((8 * ROWS, 2 * HD), BF16),
            pltpu.VMEM((8 * ROWS, 2 * HD), BF16),
            pltpu.VMEM((NZ * ROWS, 2 * HD), F32),
            pltpu.VMEM((16, PART, HD), BF16),
            pltpu.VMEM((16, 1, HD), F32),
            pltpu.VMEM((16, PART, HD), BF16),
            pltpu.VMEM((16, 1, HD), F32),
            pltpu.VMEM((16, PART, HD), BF16),
            pltpu.VMEM((16, 1, HD), F32),
            pltpu.VMEM((16, PART, HD), BF16),
            pltpu.VMEM((16, 1, HD), F32),
            dma((6,)),
            dma((8,)),
            dma((2,)),
            dma((32,)),
            dma((3,)),
            dma((3,)),
            dma((2,)),
            dma((8,)),
            dma((2,)),
            dma((8,)),
            dma((4,)),
            dma((4,)),
            dma((4,)),
            dma((4,)),
            dma(()),
            dma(()),
            dma(()),
            dma(()),
            pltpu.SemaphoreType.REGULAR,
        ],
        compiler_params=pltpu.CompilerParams(
            collective_id=0, has_side_effects=True, vmem_limit_bytes=40 * 1024 * 1024
        ),
        name="layer",
    )(*args)


def solution(mesh):
    return jax.shard_map(
        on_device,
        mesh=mesh,
        in_specs=(
            P("seq", None),
            P(None, "head"),
            P(None, "head"),
            P(None, "head"),
            P("head", None),
            P(),
        ),
        out_specs=P(("seq", "head"), None),
        check_vma=False,
    )
```

```python
import functools
import math

import jax
import jax.numpy as jnp
from jax import lax
from jax.experimental import pallas as pl
from jax.experimental.pallas import tpu as pltpu
from jax.sharding import PartitionSpec as P

MESH = pl.DeviceIdType.MESH
HD = 128
EPS = 1e-06
ROWS = 192
PART = 48
NZ = 8
F32 = jnp.float32
BF16 = jnp.bfloat16


def unit_rows(raw):
    return (raw * lax.rsqrt(jnp.mean(raw * raw, axis=-1, keepdims=True) + EPS)).astype(BF16)


class Gather:
    ORDER = (0, -1, 1, 2)

    def __init__(self, own, view, place, x_first, number, sems, first_target, target):
        self.own, self.view, self.place, self.x_first, self.number = own, view, place, x_first, number
        self.d_recv, self.send_sem, self.recv_sem = sems
        self.first_target, self.target = first_target, target
        self.table = []
        for i in self.ORDER:
            self.table += [(i, 0, None, 1), (i, 0, None, -1), (i, -1, 0, 1), (i, 1, 1, -1)]

    def at(self, i, j):
        x, y = self.place
        dx, dy = (i, j) if self.x_first else (j, i)
        return lax.rem(x + dx + 8, 4), lax.rem(y + dy + 8, 4)

    def first(self, n, received=False):
        at = self.at(-n, 0) if received else self.place
        return pltpu.make_async_remote_copy(
            src_ref=self.own,
            dst_ref=self.view(*at, None),
            send_sem=self.send_sem.at[self.number],
            recv_sem=self.d_recv.at[self.number * 4 + n],
            device_id=self.first_target(*self.at(n, 0)),
            device_id_type=MESH,
        )

    def copy(self, k, received):
        i, j, part, step = self.table[k]
        ref = self.view(*self.at(i, j - step if received else j), part)
        return self.along(k, ref, self.at(0, step))

    def along(self, k, ref, to):
        return pltpu.make_async_remote_copy(
            src_ref=ref,
            dst_ref=ref,
            send_sem=self.send_sem.at[self.number],
            recv_sem=self.recv_sem.at[self.number * 16 + k],
            device_id=self.target(*to),
            device_id_type=MESH,
        )

    def first_got(self, i):
        self.first((-i) % 4, True).wait_recv()

    def start(self, *ks):
        for k in ks:
            self.copy(k, False).start()

    def got(self, *ks):
        for k in ks:
            self.copy(k, True).wait_recv()

    def sent(self, ref):
        self.along(0, ref, self.at(0, 1)).wait_send()


def kernel(
    tok_hbm, wq_hbm, wk_hbm, wv_hbm, wo_hbm, temper_hbm, out_ref,
    temper, tok, wq, wkv, wall, qst, kvst, qbuf, kv_a, kv_b, acc,
    xo, xt, go, gt, so, st, ro, rt,
    load_sem, d_recv, g_send, g_recv, m_send, m_recv, w_send, w_recv, x_send, x_recv,
    q_send, q_recv, f_send, f_recv, o_send, o_recv, t_send, t_recv, ready,
):
    s, h = lax.axis_index("seq"), lax.axis_index("head")
    x, y, zl = lax.div(s, 32), lax.rem(lax.div(s, 8), 4), lax.rem(s, 8)
    zh, c = lax.div(h, 2), lax.rem(h, 2)
    p = lax.rem(zl, 2)
    near = lax.div(zl, 4)
    other = h + 1 - 2 * c
    across = lax.rem(h + 2, 4)
    column = s - zl
    mine = c == p
    z_first = jnp.where(mine, zl, zl + 1 - 2 * p)
    h_first = jnp.where(mine, h, other)

    def rdma(src, dst, send, recv, dev):
        return pltpu.make_async_remote_copy(
            src_ref=src, dst_ref=dst, send_sem=send, recv_sem=recv, device_id=dev, device_id_type=MESH
        )

    barrier = pltpu.get_barrier_semaphore()

    def plane(px, py):
        return ((px * 4 + py) * 8 + zl, h)

    def first_plane(px, py):
        return ((px * 4 + py) * 8 + z_first, h_first)

    def greet(dev):
        pl.semaphore_signal(barrier, inc=1, device_id=dev, device_id_type=MESH)

    def greet_plane(where):
        for n in (1, 3, 2):
            greet(where(lax.rem(x + n, 4), y))
            greet(where(x, lax.rem(y + n, 4)))

    q_self = jnp.logical_and(mine, near == c)

    @pl.when(jnp.logical_not(mine))
    def _():
        greet_plane(first_plane)
        greet(first_plane(x, y))

    greet_plane(plane)
    greet((s, other))
    greet((s, across))
    for n in range(4):

        @pl.when(jnp.logical_not(jnp.logical_and(q_self, c * 4 + n == zl)))
        def _():
            greet((column + c * 4 + n, zh * 2 + p))

    loads = [
        pltpu.make_async_copy(src, dst, load_sem.at[i])
        for i, (src, dst) in enumerate(
            [
                (tok_hbm, tok),
                (wk_hbm, wkv.at[:, pl.ds(0, HD)]),
                (wv_hbm, wkv.at[:, pl.ds(HD, HD)]),
                (wq_hbm, wq),
                (wo_hbm, wall.at[pl.ds(pl.multiple_of(h * HD, HD), HD)]),
                (temper_hbm, temper),
            ]
        )
    ]
    for load in loads:
        load.start()

    acc[...] = jnp.zeros_like(acc)

    half_rows = ROWS // 2

    def rows_of(at, part):
        if part is None:
            return pl.ds(pl.multiple_of(at * half_rows, half_rows), half_rows)
        return pl.ds(pl.multiple_of(at * half_rows + part * PART, PART), PART)

    def a_view(px, py, part):
        return kv_a.at[rows_of(py * 4 + px, part)]

    def b_view(px, py, part):
        return kv_b.at[rows_of(px * 4 + py, part)]

    sems = (d_recv, g_send, g_recv)
    along_x = Gather(kvst.at[pl.ds(0, half_rows)], a_view, (x, y), True, 0, sems, first_plane, plane)
    along_y = Gather(kvst.at[pl.ds(half_rows, half_rows)], b_view, (x, y), False, 1, sems, first_plane, plane)
    gathers = (along_x, along_y)

    def head_rows(head):
        return wall.at[pl.ds(pl.multiple_of(head * HD, HD), HD)]

    def w_piece(head, px):
        first = pl.multiple_of(head * HD + lax.rem(px, 2) * 64, 64)
        lanes = pl.multiple_of((y * 2 + lax.div(px, 2)) * 128, 128)
        return wall.at[pl.ds(first, 64), pl.ds(lanes, 128)]

    def w_row(head, py):
        return wall.at[pl.ds(pl.multiple_of(head * HD, HD), HD), pl.ds(pl.multiple_of(py * 256, 256), 256)]

    def w_share_x(n, received=False):
        ref = w_piece(across, lax.rem(x + 4 - n, 4) if received else x)
        return rdma(ref, ref, w_send.at[0], w_recv.at[n], plane(lax.rem(x + n, 4), y))

    def w_share_y(n, received=False):
        ref = w_row(across, lax.rem(y + 4 - n, 4) if received else y)
        return rdma(ref, ref, w_send.at[1], w_recv.at[4 + n], plane(x, lax.rem(y + n, 4)))

    w_across = rdma(w_piece(h, x), w_piece(h, x), m_send.at[0], m_recv.at[0], (s, across))
    w_across_in = rdma(w_piece(across, x), w_piece(across, x), m_send.at[0], m_recv.at[0], (s, across))
    w_other = rdma(head_rows(h), head_rows(h), m_send.at[1], m_recv.at[1], (s, other))
    w_other_in = rdma(head_rows(other), head_rows(other), m_send.at[1], m_recv.at[1], (s, other))
    far_other = lax.rem(other + 2, 4)
    w_last = rdma(head_rows(across), head_rows(across), m_send.at[2], m_recv.at[2], (s, other))
    w_last_in = rdma(head_rows(far_other), head_rows(far_other), m_send.at[2], m_recv.at[2], (s, other))

    loads[0].wait()
    loads[1].wait()
    loads[2].wait()
    raw = jnp.dot(tok[...], wkv[...], preferred_element_type=F32)
    both = jnp.concatenate([unit_rows(raw[:, :HD]), raw[:, HD:].astype(BF16)], axis=1)
    kvst[...] = both

    @pl.when(mine)
    def _():
        kv_a[rows_of(y * 4 + x, None)] = both[:half_rows]
        kv_b[rows_of(x * 4 + y, None)] = both[half_rows:]
        pl.semaphore_wait(barrier, 12 - jnp.where(near == c, 1, 0))

    @pl.when(jnp.logical_not(mine))
    def _():
        pl.semaphore_wait(barrier, 19)

    def give_first(g):
        for n in (1, 3, 2):
            g.first(n).start()

        @pl.when(jnp.logical_not(mine))
        def _():
            g.first(0).start()

        @pl.when(mine)
        def _():
            g.start(0, 1)

    give_first(along_x)
    give_first(along_y)
    loads[4].wait()
    w_across.start()
    loads[3].wait()
    query_unit = unit_rows(jnp.dot(tok[...], wq[...], preferred_element_type=F32))
    qst[...] = query_unit

    def q_view(u):
        return qbuf.at[pl.ds(pl.multiple_of(u * ROWS, ROWS), ROWS)]

    half, bit = lax.div(zl, 4), lax.rem(lax.div(zl, 2), 2)
    q_targets = (half * 2 + bit, half * 2 + 1 - bit, 2 - half * 2 + bit, 3 - half * 2 - bit)

    def q_copy(n):
        return rdma(
            qst,
            q_view(zl),
            q_send.at[n],
            q_recv.at[lax.rem(zl, 4)],
            (column + c + 2 * q_targets[n], zh * 2 + near),
        )

    @pl.when(q_self)
    def _():
        qbuf[pl.ds(pl.multiple_of(zl * ROWS, ROWS), ROWS)] = query_unit

    @pl.when(jnp.logical_not(q_self))
    def _():
        q_copy(0).start()

    q_copy(1).start()
    loads[5].wait()
    w_other.start()

    @pl.when(jnp.logical_not(mine))
    def _():
        for g in gathers:
            g.first_got(0)
            g.start(0, 1)

    for t, i in ((1, -1), (2, 1), (3, 2)):
        for g in gathers:
            g.first_got(i)
            g.start(4 * t, 4 * t + 1)

    for n in (2, 3):
        q_copy(n).start()

    def relay(g, t):
        g.got(4 * t)
        g.start(4 * t + 2)
        g.got(4 * t + 1)
        g.start(4 * t + 3)

    def unit_at(k):
        return k + near * (7 - 2 * k)

    def q_arrived(k):
        u = unit_at(k)
        slot = lax.rem(u, 4)
        first_core = (near == c) if k < 4 else (near != c)
        forward = rdma(q_view(u), q_view(u), f_send.at[slot], f_recv.at[slot], (s, other))
        direct = rdma(q_view(u), q_view(u), q_send.at[0], q_recv.at[slot], (s, other))

        @pl.when(first_core)
        def _():
            if k < 4:

                @pl.when(jnp.logical_not(jnp.logical_and(q_self, u == zl)))
                def _():
                    direct.wait_recv()
            else:
                direct.wait_recv()
            forward.start()

        @pl.when(jnp.logical_not(first_core))
        def _():
            forward.wait_recv()

    scale = temper[zh * 2 + p] * F32(math.log2(math.e) / math.sqrt(HD))

    ones = jnp.ones((4 * ROWS, HD), BF16)

    def piece(half, d):
        q0 = pl.multiple_of(half * (4 * ROWS), 4 * ROWS)
        a0 = pl.multiple_of(lax.rem(y + d, 4) * (2 * ROWS), 2 * ROWS)
        b0 = pl.multiple_of(lax.rem(x + d, 4) * (2 * ROWS), 2 * ROWS)
        both_k = jnp.concatenate([kv_a[pl.ds(a0, 2 * ROWS), :HD], kv_b[pl.ds(b0, 2 * ROWS), :HD]], axis=0)
        both_v = jnp.concatenate([kv_a[pl.ds(a0, 2 * ROWS), HD:], kv_b[pl.ds(b0, 2 * ROWS), HD:]], axis=0)
        score = lax.dot_general(
            qbuf[pl.ds(q0, 4 * ROWS)], both_k, (((1,), (1,)), ((), ())), preferred_element_type=F32
        )
        weight = jnp.exp2(score * scale).astype(BF16)
        value_block = jnp.concatenate([both_v, ones], axis=1)
        acc[pl.ds(q0, 4 * ROWS)] += jnp.dot(weight, value_block, preferred_element_type=F32)

    lane = lax.broadcasted_iota(jnp.int32, (PART, HD), 1)
    row = lax.broadcasted_iota(jnp.int32, (PART, HD), 0)
    diagonal = lane == row
    slot = (zh * 2 + p) * 4 + lax.div(zl, 2)

    def part_rows(core, i):
        return pl.ds(pl.multiple_of(core * (4 * ROWS) + i * PART, PART), PART)

    def give_copies(n):
        at = pl.ds(pl.multiple_of(n * 4, 4), 4)
        return (
            rdma(xo.at[at], go.at[at], x_send.at[0], x_recv.at[n], (s, other)),
            rdma(xt.at[at], gt.at[at], x_send.at[1], x_recv.at[4 + n], (s, other)),
        )

    def block_of(core, i):
        block = acc[part_rows(core, i)]
        return block[:, :HD], jnp.sum(jnp.where(diagonal, block[:, HD:], 0.0), axis=0, keepdims=True)

    def turn(n):
        return lax.rem(n + zl, 4)

    def give(m, carry):
        n = turn(m)

        def one(k, inner):
            i = n * 4 + k
            summed, xt[i] = block_of(1 - c, i)
            xo[i] = summed.astype(BF16)
            return inner

        lax.fori_loop(0, 4, one, 0)
        for copy in give_copies(n):
            copy.start()
        return carry

    def o_copy(i):
        dev = (column + c * 4 + lax.div(i, 4), lax.rem(i, 4))
        return (
            rdma(so.at[i], ro.at[slot], o_send, o_recv, dev),
            rdma(st.at[i], rt.at[slot], t_send, t_recv, dev),
        )

    def o_self(i):
        return jnp.logical_and(c * 4 + lax.div(i, 4) == zl, lax.rem(i, 4) == h)

    def settle(m, carry):
        n = turn(m)
        for copy in give_copies(n):
            copy.wait_recv()

        def one(k, inner):
            i = n * 4 + k
            summed, total = block_of(c, i)
            summed, total = (summed + go[i].astype(F32)).astype(BF16), total + gt[i]
            so[i], st[i] = summed, total

            @pl.when(o_self(i))
            def _():
                ro[slot], rt[slot] = summed, total

            @pl.when(jnp.logical_not(o_self(i)))
            def _():
                for copy in o_copy(i):
                    copy.start()

            return inner

        lax.fori_loop(0, 4, one, 0)
        return carry

    def step(i, carry):
        def at(n, events):
            @pl.when(i == n)
            def _():
                events()

        def before_1():
            for t in range(4):
                for g in gathers:
                    relay(g, t)
            w_across_in.wait_recv()
            for n in (1, 3, 2):
                w_share_x(n).start()

        def before_3():
            for g in gathers:
                g.got(2, 3, 6, 7, 10, 11, 14, 15)
            for n in (1, 3, 2):
                w_share_x(n, True).wait_recv()
            for n in (1, 3, 2):
                w_share_y(n).start()

        def before_4():
            @pl.when(near != c)
            def _():
                lax.fori_loop(0, 4, give, 0)

            for k in range(4, 8):
                q_arrived(k)
            pl.semaphore_signal(ready, inc=1, device_id=(s, across), device_id_type=MESH)

        def before_5():
            for n in (1, 3, 2):
                w_share_y(n, True).wait_recv()
            w_last.start()

        def before_6():
            pl.semaphore_wait(ready, 1)

            @pl.when(near == c)
            def _():
                lax.fori_loop(0, 4, settle, 0)

        at(1, before_1)
        at(3, before_3)
        at(4, before_4)
        at(5, before_5)
        at(6, before_6)
        r = lax.rem(i, 4)
        piece(
            jnp.where(i < 4, near, 1 - near),
            jnp.where(r == 0, 0, jnp.where(r == 1, 3, jnp.where(r == 2, 1, 2))),
        )
        return carry

    for k in range(4):
        q_arrived(k)
    lax.fori_loop(0, 8, step, 0)

    @pl.when(near == c)
    def _():
        lax.fori_loop(0, 4, give, 0)

    @pl.when(near != c)
    def _():
        lax.fori_loop(0, 4, settle, 0)

    for g, ref in ((along_x, kv_a), (along_y, kv_b)):
        @pl.when(mine)
        def _():
            g.sent(ref.at[pl.ds(0, 15 * half_rows)])

        @pl.when(jnp.logical_not(mine))
        def _():
            g.sent(ref)

    for copy in (w_across, w_other, w_last):
        copy.wait_send()
    three_pieces = wall.at[pl.ds(0, 64), pl.ds(0, 384)]
    three_rows = wall.at[pl.ds(0, HD), pl.ds(0, 768)]
    rdma(three_pieces, three_pieces, w_send.at[0], w_recv.at[1], plane(lax.rem(x + 1, 4), y)).wait_send()
    rdma(three_rows, three_rows, w_send.at[1], w_recv.at[5], plane(x, lax.rem(y + 1, 4))).wait_send()
    rdma(xo, go, x_send.at[0], x_recv.at[0], (s, other)).wait_send()
    rdma(xt, gt, x_send.at[1], x_recv.at[4], (s, other)).wait_send()

    @pl.when(jnp.logical_not(q_self))
    def _():
        q_copy(0).wait_send()

    for n in (1, 2, 3):
        q_copy(n).wait_send()

    def forwarded(i, carry):
        rdma(q_view(c * 4 + i), q_view(c * 4 + i), f_send.at[i], f_recv.at[i], (s, other)).wait_send()
        return carry

    lax.fori_loop(0, 4, forwarded, 0)

    w_other_in.wait_recv()
    w_last_in.wait_recv()

    def all_parts(count):
        at = pl.ds(0, count)
        return (
            rdma(so.at[at], ro.at[at], o_send, o_recv, (s, other)),
            rdma(st.at[at], rt.at[at], t_send, t_recv, (s, other)),
        )

    @pl.when(near == c)
    def _():
        for copy in all_parts(15):
            copy.wait_recv()

    @pl.when(near != c)
    def _():
        for copy in all_parts(16):
            copy.wait_recv()

    attended = []
    for head in range(4):
        summed = sum(ro[head * 4 + j].astype(F32) for j in range(4))
        total = sum(rt[head * 4 + j] for j in range(4))
        total = jnp.sum(jnp.where(diagonal, jnp.broadcast_to(total, (PART, HD)), 0.0), axis=1, keepdims=True)
        attended.append((summed / total).astype(BF16))
    out_ref[...] = jnp.dot(
        jnp.concatenate(attended, axis=1), wall[...], preferred_element_type=F32
    ).astype(BF16)

    @pl.when(near == c)
    def _():
        for copy in all_parts(15):
            copy.wait_send()

    @pl.when(near != c)
    def _():
        for copy in all_parts(16):
            copy.wait_send()


def on_device(tokens, w_query, w_key, w_value, w_out, temper):
    dma = pltpu.SemaphoreType.DMA
    args = [
        pltpu.with_memory_space_constraint(a, pltpu.HBM)
        for a in (tokens, w_query, w_key, w_value, w_out, temper)
    ]
    d_model = tokens.shape[1]
    return pl.pallas_call(
        kernel,
        out_shape=jax.ShapeDtypeStruct((PART, d_model), BF16),
        in_specs=[pl.BlockSpec(memory_space=pltpu.HBM)] * 6,
        out_specs=pl.BlockSpec(memory_space=pltpu.VMEM),
        scratch_shapes=[
            pltpu.SMEM((4,), F32),
            pltpu.VMEM((ROWS, d_model), BF16),
            pltpu.VMEM((d_model, HD), BF16),
            pltpu.VMEM((d_model, 2 * HD), BF16),
            pltpu.VMEM((4 * HD, d_model), BF16),
            pltpu.VMEM((ROWS, HD), BF16),
            pltpu.VMEM((ROWS, 2 * HD), BF16),
            pltpu.VMEM((NZ * ROWS, HD), BF16),
            pltpu.VMEM((8 * ROWS, 2 * HD), BF16),
            pltpu.VMEM((8 * ROWS, 2 * HD), BF16),
            pltpu.VMEM((NZ * ROWS, 2 * HD), F32),
            pltpu.VMEM((16, PART, HD), BF16),
            pltpu.VMEM((16, 1, HD), F32),
            pltpu.VMEM((16, PART, HD), BF16),
            pltpu.VMEM((16, 1, HD), F32),
            pltpu.VMEM((16, PART, HD), BF16),
            pltpu.VMEM((16, 1, HD), F32),
            pltpu.VMEM((16, PART, HD), BF16),
            pltpu.VMEM((16, 1, HD), F32),
            dma((6,)),
            dma((8,)),
            dma((2,)),
            dma((32,)),
            dma((3,)),
            dma((3,)),
            dma((2,)),
            dma((8,)),
            dma((2,)),
            dma((8,)),
            dma((4,)),
            dma((4,)),
            dma((4,)),
            dma((4,)),
            dma(()),
            dma(()),
            dma(()),
            dma(()),
            pltpu.SemaphoreType.REGULAR,
        ],
        compiler_params=pltpu.CompilerParams(
            collective_id=0, has_side_effects=True, vmem_limit_bytes=40 * 1024 * 1024
        ),
        name="layer",
    )(*args)


def solution(mesh):
    return jax.shard_map(
        on_device,
        mesh=mesh,
        in_specs=(
            P("seq", None),
            P(None, "head"),
            P(None, "head"),
            P(None, "head"),
            P("head", None),
            P(),
        ),
        out_specs=P(("seq", "head"), None),
        check_vma=False,
    )
```

```python
import functools
import math

import jax
import jax.numpy as jnp
from jax import lax
from jax.experimental import pallas as pl
from jax.experimental.pallas import tpu as pltpu
from jax.sharding import PartitionSpec as P

MESH = pl.DeviceIdType.MESH
HD = 128
EPS = 1e-06
ROWS = 192
PART = 48
NZ = 8
F32 = jnp.float32
BF16 = jnp.bfloat16


def unit_rows(raw):
    return (raw * lax.rsqrt(jnp.mean(raw * raw, axis=-1, keepdims=True) + EPS)).astype(BF16)


class Gather:
    ORDER = (0, -1, 1, 2)

    def __init__(self, own, view, place, x_first, number, sems, target):
        self.own, self.view, self.place, self.x_first, self.number = own, view, place, x_first, number
        self.d_recv, self.send_sem, self.recv_sem = sems
        self.target = target
        self.table = []
        for i in self.ORDER:
            self.table += [(i, 0, None, 1), (i, 0, None, -1), (i, -1, 0, 1), (i, 1, 1, -1)]

    def at(self, i, j):
        x, y = self.place
        dx, dy = (i, j) if self.x_first else (j, i)
        return lax.rem(x + dx + 8, 4), lax.rem(y + dy + 8, 4)

    def first(self, n, received=False):
        at = self.at(-n, 0) if received else self.place
        return pltpu.make_async_remote_copy(
            src_ref=self.own,
            dst_ref=self.view(*at, None),
            send_sem=self.send_sem.at[self.number],
            recv_sem=self.d_recv.at[self.number * 4 + n],
            device_id=self.target(*self.at(n, 0)),
            device_id_type=MESH,
        )

    def copy(self, k, received):
        i, j, part, step = self.table[k]
        ref = self.view(*self.at(i, j - step if received else j), part)
        return self.along(k, ref, self.at(0, step))

    def along(self, k, ref, to):
        return pltpu.make_async_remote_copy(
            src_ref=ref,
            dst_ref=ref,
            send_sem=self.send_sem.at[self.number],
            recv_sem=self.recv_sem.at[self.number * 16 + k],
            device_id=self.target(*to),
            device_id_type=MESH,
        )

    def first_got(self, i):
        self.first((-i) % 4, True).wait_recv()

    def start(self, *ks):
        for k in ks:
            self.copy(k, False).start()

    def got(self, *ks):
        for k in ks:
            self.copy(k, True).wait_recv()

    def sent(self, ref):
        self.along(0, ref, self.at(0, 1)).wait_send()


def kernel(
    tok_hbm, wq_hbm, wk_hbm, wv_hbm, wo_hbm, temper_hbm, out_ref,
    temper, tok, wq, wkv, wall, qst, kvst, kvown, qbuf, kv_a, kv_b, acc,
    xo, xt, go, gt, so, st, ro, rt,
    load_sem, d_recv, g_send, g_recv, m_send, m_recv, w_send, w_recv, x_send, x_recv,
    q_send, q_recv, f_send, f_recv, o_send, o_recv, t_send, t_recv, ready,
):
    s, h = lax.axis_index("seq"), lax.axis_index("head")
    x, y, zl = lax.div(s, 32), lax.rem(lax.div(s, 8), 4), lax.rem(s, 8)
    zh, c = lax.div(h, 2), lax.rem(h, 2)
    p = lax.rem(zl, 2)
    near = lax.div(zl, 4)
    other = h + 1 - 2 * c
    across = lax.rem(h + 2, 4)
    column = s - zl
    mine = c == p

    def rdma(src, dst, send, recv, dev):
        return pltpu.make_async_remote_copy(
            src_ref=src, dst_ref=dst, send_sem=send, recv_sem=recv, device_id=dev, device_id_type=MESH
        )

    barrier = pltpu.get_barrier_semaphore()

    def plane(px, py):
        return ((px * 4 + py) * 8 + zl, h)

    def greet(dev):
        pl.semaphore_signal(barrier, inc=1, device_id=dev, device_id_type=MESH)

    q_self = jnp.logical_and(mine, near == c)

    swap_to = (s + 1 - 2 * p, other)

    @pl.when(jnp.logical_not(mine))
    def _():
        greet(swap_to)

    for n in (1, 3, 2):
        greet(plane(lax.rem(x + n, 4), y))
        greet(plane(x, lax.rem(y + n, 4)))
    greet((s, other))
    greet((s, across))
    for n in range(4):

        @pl.when(jnp.logical_not(jnp.logical_and(q_self, c * 4 + n == zl)))
        def _():
            greet((column + c * 4 + n, zh * 2 + p))

    loads = [
        pltpu.make_async_copy(src, dst, load_sem.at[i])
        for i, (src, dst) in enumerate(
            [
                (tok_hbm, tok),
                (wk_hbm, wkv.at[:, pl.ds(0, HD)]),
                (wv_hbm, wkv.at[:, pl.ds(HD, HD)]),
                (wq_hbm, wq),
                (wo_hbm, wall.at[pl.ds(pl.multiple_of(h * HD, HD), HD)]),
                (temper_hbm, temper),
            ]
        )
    ]
    for load in loads:
        load.start()

    acc[...] = jnp.zeros_like(acc)

    half_rows = ROWS // 2

    def rows_of(at, part):
        if part is None:
            return pl.ds(pl.multiple_of(at * half_rows, half_rows), half_rows)
        return pl.ds(pl.multiple_of(at * half_rows + part * PART, PART), PART)

    def a_view(px, py, part):
        return kv_a.at[rows_of(py * 4 + px, part)]

    def b_view(px, py, part):
        return kv_b.at[rows_of(px * 4 + py, part)]

    sems = (d_recv, g_send, g_recv)
    along_x = Gather(kvown.at[pl.ds(0, half_rows)], a_view, (x, y), True, 0, sems, plane)
    along_y = Gather(kvown.at[pl.ds(half_rows, half_rows)], b_view, (x, y), False, 1, sems, plane)
    gathers = (along_x, along_y)

    def head_rows(head):
        return wall.at[pl.ds(pl.multiple_of(head * HD, HD), HD)]

    def w_piece(head, px):
        first = pl.multiple_of(head * HD + lax.rem(px, 2) * 64, 64)
        lanes = pl.multiple_of((y * 2 + lax.div(px, 2)) * 128, 128)
        return wall.at[pl.ds(first, 64), pl.ds(lanes, 128)]

    def w_row(head, py):
        return wall.at[pl.ds(pl.multiple_of(head * HD, HD), HD), pl.ds(pl.multiple_of(py * 256, 256), 256)]

    def w_share_x(n, received=False):
        ref = w_piece(across, lax.rem(x + 4 - n, 4) if received else x)
        return rdma(ref, ref, w_send.at[0], w_recv.at[n], plane(lax.rem(x + n, 4), y))

    def w_share_y(n, received=False):
        ref = w_row(across, lax.rem(y + 4 - n, 4) if received else y)
        return rdma(ref, ref, w_send.at[1], w_recv.at[4 + n], plane(x, lax.rem(y + n, 4)))

    w_across = rdma(w_piece(h, x), w_piece(h, x), m_send.at[0], m_recv.at[0], (s, across))
    w_across_in = rdma(w_piece(across, x), w_piece(across, x), m_send.at[0], m_recv.at[0], (s, across))
    w_other = rdma(head_rows(h), head_rows(h), m_send.at[1], m_recv.at[1], (s, other))
    w_other_in = rdma(head_rows(other), head_rows(other), m_send.at[1], m_recv.at[1], (s, other))
    far_other = lax.rem(other + 2, 4)
    w_last = rdma(head_rows(across), head_rows(across), m_send.at[2], m_recv.at[2], (s, other))
    w_last_in = rdma(head_rows(far_other), head_rows(far_other), m_send.at[2], m_recv.at[2], (s, other))

    loads[0].wait()
    loads[1].wait()
    loads[2].wait()
    raw = jnp.dot(tok[...], wkv[...], preferred_element_type=F32)
    both = jnp.concatenate([unit_rows(raw[:, :HD]), raw[:, HD:].astype(BF16)], axis=1)
    kv_swap = rdma(kvst, kvown, m_send.at[3], m_recv.at[3], swap_to)

    def give_first():
        for g in gathers:
            for n in (1, 3, 2):
                g.first(n).start()
        for g in gathers:
            g.start(0, 1)

    def place_own(block):
        kv_a[rows_of(y * 4 + x, None)] = block[:half_rows]
        kv_b[rows_of(x * 4 + y, None)] = block[half_rows:]

    @pl.when(mine)
    def _():
        kvown[...] = both
        place_own(both)
        pl.semaphore_wait(barrier, 12 - jnp.where(near == c, 1, 0))
        give_first()

    @pl.when(jnp.logical_not(mine))
    def _():
        kvst[...] = both
        pl.semaphore_wait(barrier, 13)
        kv_swap.start()

    loads[4].wait()
    w_across.start()
    loads[3].wait()
    query_unit = unit_rows(jnp.dot(tok[...], wq[...], preferred_element_type=F32))
    qst[...] = query_unit

    def q_view(u):
        return qbuf.at[pl.ds(pl.multiple_of(u * ROWS, ROWS), ROWS)]

    half, bit = lax.div(zl, 4), lax.rem(lax.div(zl, 2), 2)
    q_targets = (half * 2 + bit, half * 2 + 1 - bit, 2 - half * 2 + bit, 3 - half * 2 - bit)

    def q_copy(n):
        return rdma(
            qst,
            q_view(zl),
            q_send.at[n],
            q_recv.at[lax.rem(zl, 4)],
            (column + c + 2 * q_targets[n], zh * 2 + near),
        )

    @pl.when(q_self)
    def _():
        qbuf[pl.ds(pl.multiple_of(zl * ROWS, ROWS), ROWS)] = query_unit

    @pl.when(jnp.logical_not(q_self))
    def _():
        q_copy(0).start()

    q_copy(1).start()
    loads[5].wait()
    w_other.start()

    @pl.when(jnp.logical_not(mine))
    def _():
        kv_swap.wait_recv()
        place_own(kvown[...])
        give_first()

    for t, i in ((1, -1), (2, 1), (3, 2)):
        for g in gathers:
            g.first_got(i)
            g.start(4 * t, 4 * t + 1)

    for n in (2, 3):
        q_copy(n).start()

    def relay(g, t):
        g.got(4 * t)
        g.start(4 * t + 2)
        g.got(4 * t + 1)
        g.start(4 * t + 3)

    def unit_at(k):
        return k + near * (7 - 2 * k)

    def q_arrived(k):
        u = unit_at(k)
        slot = lax.rem(u, 4)
        first_core = (near == c) if k < 4 else (near != c)
        forward = rdma(q_view(u), q_view(u), f_send.at[slot], f_recv.at[slot], (s, other))
        direct = rdma(q_view(u), q_view(u), q_send.at[0], q_recv.at[slot], (s, other))

        @pl.when(first_core)
        def _():
            if k < 4:

                @pl.when(jnp.logical_not(jnp.logical_and(q_self, u == zl)))
                def _():
                    direct.wait_recv()
            else:
                direct.wait_recv()
            forward.start()

        @pl.when(jnp.logical_not(first_core))
        def _():
            forward.wait_recv()

    scale = temper[zh * 2 + p] * F32(math.log2(math.e) / math.sqrt(HD))

    ones = jnp.ones((4 * ROWS, HD), BF16)

    def piece(half, d):
        q0 = pl.multiple_of(half * (4 * ROWS), 4 * ROWS)
        a0 = pl.multiple_of(lax.rem(y + d, 4) * (2 * ROWS), 2 * ROWS)
        b0 = pl.multiple_of(lax.rem(x + d, 4) * (2 * ROWS), 2 * ROWS)
        both_k = jnp.concatenate([kv_a[pl.ds(a0, 2 * ROWS), :HD], kv_b[pl.ds(b0, 2 * ROWS), :HD]], axis=0)
        both_v = jnp.concatenate([kv_a[pl.ds(a0, 2 * ROWS), HD:], kv_b[pl.ds(b0, 2 * ROWS), HD:]], axis=0)
        score = lax.dot_general(
            qbuf[pl.ds(q0, 4 * ROWS)], both_k, (((1,), (1,)), ((), ())), preferred_element_type=F32
        )
        weight = jnp.exp2(score * scale).astype(BF16)
        value_block = jnp.concatenate([both_v, ones], axis=1)
        acc[pl.ds(q0, 4 * ROWS)] += jnp.dot(weight, value_block, preferred_element_type=F32)

    lane = lax.broadcasted_iota(jnp.int32, (PART, HD), 1)
    row = lax.broadcasted_iota(jnp.int32, (PART, HD), 0)
    diagonal = lane == row
    slot = (zh * 2 + p) * 4 + lax.div(zl, 2)

    def part_rows(core, i):
        return pl.ds(pl.multiple_of(core * (4 * ROWS) + i * PART, PART), PART)

    def give_copies(n):
        at = pl.ds(pl.multiple_of(n * 4, 4), 4)
        return (
            rdma(xo.at[at], go.at[at], x_send.at[0], x_recv.at[n], (s, other)),
            rdma(xt.at[at], gt.at[at], x_send.at[1], x_recv.at[4 + n], (s, other)),
        )

    def block_of(core, i):
        block = acc[part_rows(core, i)]
        return block[:, :HD], jnp.sum(jnp.where(diagonal, block[:, HD:], 0.0), axis=0, keepdims=True)

    def turn(n):
        return lax.rem(n + zl, 4)

    def give(m, carry):
        n = turn(m)

        def one(k, inner):
            i = n * 4 + k
            summed, xt[i] = block_of(1 - c, i)
            xo[i] = summed.astype(BF16)
            return inner

        lax.fori_loop(0, 4, one, 0)
        for copy in give_copies(n):
            copy.start()
        return carry

    def o_copy(i):
        dev = (column + c * 4 + lax.div(i, 4), lax.rem(i, 4))
        return (
            rdma(so.at[i], ro.at[slot], o_send, o_recv, dev),
            rdma(st.at[i], rt.at[slot], t_send, t_recv, dev),
        )

    def o_self(i):
        return jnp.logical_and(c * 4 + lax.div(i, 4) == zl, lax.rem(i, 4) == h)

    def settle(m, carry):
        n = turn(m)
        for copy in give_copies(n):
            copy.wait_recv()

        def one(k, inner):
            i = n * 4 + k
            summed, total = block_of(c, i)
            summed, total = (summed + go[i].astype(F32)).astype(BF16), total + gt[i]
            so[i], st[i] = summed, total

            @pl.when(o_self(i))
            def _():
                ro[slot], rt[slot] = summed, total

            @pl.when(jnp.logical_not(o_self(i)))
            def _():
                for copy in o_copy(i):
                    copy.start()

            return inner

        lax.fori_loop(0, 4, one, 0)
        return carry

    def step(i, carry):
        def at(n, events):
            @pl.when(i == n)
            def _():
                events()

        def before_1():
            for t in (1, 2, 3):
                for g in gathers:
                    relay(g, t)
            w_across_in.wait_recv()
            for n in (1, 3, 2):
                w_share_x(n).start()

        def before_3():
            for k in range(4, 8):
                q_arrived(k)
            pl.semaphore_signal(ready, inc=1, device_id=(s, across), device_id_type=MESH)
            for n in (1, 3, 2):
                w_share_x(n, True).wait_recv()
            for n in (1, 3, 2):
                w_share_y(n).start()

        def before_5():
            for n in (1, 3, 2):
                w_share_y(n, True).wait_recv()

        def before_6():
            for g in gathers:
                g.got(2, 3, 6, 7, 10, 11, 14, 15)

        def before_7():
            @pl.when(near != c)
            def _():
                lax.fori_loop(0, 4, give, 0)

        at(1, before_1)
        at(3, before_3)
        at(5, before_5)
        at(6, before_6)
        at(7, before_7)
        near_now = jnp.logical_or(i < 3, i == 6)
        r = jnp.where(i >= 6, 3, lax.rem(i, 3))
        piece(
            jnp.where(near_now, near, 1 - near),
            jnp.where(r == 0, 0, jnp.where(r == 1, 3, jnp.where(r == 2, 1, 2))),
        )
        return carry

    for g in gathers:
        relay(g, 0)
    for k in range(4):
        q_arrived(k)
    lax.fori_loop(0, 8, step, 0)

    @pl.when(near == c)
    def _():
        lax.fori_loop(0, 4, give, 0)

    w_last.start()
    pl.semaphore_wait(ready, 1)
    lax.fori_loop(0, 4, settle, 0)

    for g, ref in ((along_x, kv_a), (along_y, kv_b)):
        g.sent(ref.at[pl.ds(0, 15 * half_rows)])

    @pl.when(jnp.logical_not(mine))
    def _():
        kv_swap.wait_send()

    for copy in (w_across, w_other, w_last):
        copy.wait_send()
    three_pieces = wall.at[pl.ds(0, 64), pl.ds(0, 384)]
    three_rows = wall.at[pl.ds(0, HD), pl.ds(0, 768)]
    rdma(three_pieces, three_pieces, w_send.at[0], w_recv.at[1], plane(lax.rem(x + 1, 4), y)).wait_send()
    rdma(three_rows, three_rows, w_send.at[1], w_recv.at[5], plane(x, lax.rem(y + 1, 4))).wait_send()
    rdma(xo, go, x_send.at[0], x_recv.at[0], (s, other)).wait_send()
    rdma(xt, gt, x_send.at[1], x_recv.at[4], (s, other)).wait_send()

    @pl.when(jnp.logical_not(q_self))
    def _():
        q_copy(0).wait_send()

    for n in (1, 2, 3):
        q_copy(n).wait_send()

    def forwarded(i, carry):
        rdma(q_view(c * 4 + i), q_view(c * 4 + i), f_send.at[i], f_recv.at[i], (s, other)).wait_send()
        return carry

    lax.fori_loop(0, 4, forwarded, 0)

    w_other_in.wait_recv()
    w_last_in.wait_recv()

    def all_parts(count):
        at = pl.ds(0, count)
        return (
            rdma(so.at[at], ro.at[at], o_send, o_recv, (s, other)),
            rdma(st.at[at], rt.at[at], t_send, t_recv, (s, other)),
        )

    @pl.when(near == c)
    def _():
        for copy in all_parts(15):
            copy.wait_recv()

    @pl.when(near != c)
    def _():
        for copy in all_parts(16):
            copy.wait_recv()

    attended = []
    for head in range(4):
        summed = sum(ro[head * 4 + j].astype(F32) for j in range(4))
        total = sum(rt[head * 4 + j] for j in range(4))
        total = jnp.sum(jnp.where(diagonal, jnp.broadcast_to(total, (PART, HD)), 0.0), axis=1, keepdims=True)
        attended.append((summed / total).astype(BF16))
    out_ref[...] = jnp.dot(
        jnp.concatenate(attended, axis=1), wall[...], preferred_element_type=F32
    ).astype(BF16)

    @pl.when(near == c)
    def _():
        for copy in all_parts(15):
            copy.wait_send()

    @pl.when(near != c)
    def _():
        for copy in all_parts(16):
            copy.wait_send()


def on_device(tokens, w_query, w_key, w_value, w_out, temper):
    dma = pltpu.SemaphoreType.DMA
    args = [
        pltpu.with_memory_space_constraint(a, pltpu.HBM)
        for a in (tokens, w_query, w_key, w_value, w_out, temper)
    ]
    d_model = tokens.shape[1]
    return pl.pallas_call(
        kernel,
        out_shape=jax.ShapeDtypeStruct((PART, d_model), BF16),
        in_specs=[pl.BlockSpec(memory_space=pltpu.HBM)] * 6,
        out_specs=pl.BlockSpec(memory_space=pltpu.VMEM),
        scratch_shapes=[
            pltpu.SMEM((4,), F32),
            pltpu.VMEM((ROWS, d_model), BF16),
            pltpu.VMEM((d_model, HD), BF16),
            pltpu.VMEM((d_model, 2 * HD), BF16),
            pltpu.VMEM((4 * HD, d_model), BF16),
            pltpu.VMEM((ROWS, HD), BF16),
            pltpu.VMEM((ROWS, 2 * HD), BF16),
            pltpu.VMEM((ROWS, 2 * HD), BF16),
            pltpu.VMEM((NZ * ROWS, HD), BF16),
            pltpu.VMEM((8 * ROWS, 2 * HD), BF16),
            pltpu.VMEM((8 * ROWS, 2 * HD), BF16),
            pltpu.VMEM((NZ * ROWS, 2 * HD), F32),
            pltpu.VMEM((16, PART, HD), BF16),
            pltpu.VMEM((16, 1, HD), F32),
            pltpu.VMEM((16, PART, HD), BF16),
            pltpu.VMEM((16, 1, HD), F32),
            pltpu.VMEM((16, PART, HD), BF16),
            pltpu.VMEM((16, 1, HD), F32),
            pltpu.VMEM((16, PART, HD), BF16),
            pltpu.VMEM((16, 1, HD), F32),
            dma((6,)),
            dma((8,)),
            dma((2,)),
            dma((32,)),
            dma((4,)),
            dma((4,)),
            dma((2,)),
            dma((8,)),
            dma((2,)),
            dma((8,)),
            dma((4,)),
            dma((4,)),
            dma((4,)),
            dma((4,)),
            dma(()),
            dma(()),
            dma(()),
            dma(()),
            pltpu.SemaphoreType.REGULAR,
        ],
        compiler_params=pltpu.CompilerParams(
            collective_id=0, has_side_effects=True, vmem_limit_bytes=40 * 1024 * 1024
        ),
        name="layer",
    )(*args)


def solution(mesh):
    return jax.shard_map(
        on_device,
        mesh=mesh,
        in_specs=(
            P("seq", None),
            P(None, "head"),
            P(None, "head"),
            P(None, "head"),
            P("head", None),
            P(),
        ),
        out_specs=P(("seq", "head"), None),
        check_vma=False,
    )
```

```python
import functools
import math

import jax
import jax.numpy as jnp
from jax import lax
from jax.experimental import pallas as pl
from jax.experimental.pallas import tpu as pltpu
from jax.sharding import PartitionSpec as P

MESH = pl.DeviceIdType.MESH
HD = 128
EPS = 1e-06
ROWS = 192
PART = 48
NZ = 8
F32 = jnp.float32
BF16 = jnp.bfloat16


def unit_rows(raw):
    return (raw * lax.rsqrt(jnp.mean(raw * raw, axis=-1, keepdims=True) + EPS)).astype(BF16)


class Gather:
    ORDER = (0, -1, 1, 2)

    def __init__(self, own, view, place, x_first, number, sems, target):
        self.own, self.view, self.place, self.x_first, self.number = own, view, place, x_first, number
        self.d_recv, self.send_sem, self.recv_sem = sems
        self.target = target
        self.table = []
        for i in self.ORDER:
            self.table += [(i, 0, None, 1), (i, 0, None, -1), (i, -1, 0, 1), (i, 1, 1, -1)]

    def at(self, i, j):
        x, y = self.place
        dx, dy = (i, j) if self.x_first else (j, i)
        return lax.rem(x + dx + 8, 4), lax.rem(y + dy + 8, 4)

    def first(self, n, received=False):
        at = self.at(-n, 0) if received else self.place
        return pltpu.make_async_remote_copy(
            src_ref=self.own,
            dst_ref=self.view(*at, None),
            send_sem=self.send_sem.at[self.number],
            recv_sem=self.d_recv.at[self.number * 4 + n],
            device_id=self.target(*self.at(n, 0)),
            device_id_type=MESH,
        )

    def copy(self, k, received):
        i, j, part, step = self.table[k]
        ref = self.view(*self.at(i, j - step if received else j), part)
        return self.along(k, ref, self.at(0, step))

    def along(self, k, ref, to):
        return pltpu.make_async_remote_copy(
            src_ref=ref,
            dst_ref=ref,
            send_sem=self.send_sem.at[self.number],
            recv_sem=self.recv_sem.at[self.number * 16 + k],
            device_id=self.target(*to),
            device_id_type=MESH,
        )

    def first_got(self, i):
        self.first((-i) % 4, True).wait_recv()

    def start(self, *ks):
        for k in ks:
            self.copy(k, False).start()

    def got(self, *ks):
        for k in ks:
            self.copy(k, True).wait_recv()

    def sent(self, ref):
        self.along(0, ref, self.at(0, 1)).wait_send()


def kernel(
    tok_hbm, wq_hbm, wk_hbm, wv_hbm, wo_hbm, temper_hbm, out_ref,
    temper, tok, wq, wkv, wall, qst, kvst, kvown, qbuf, kv_a, kv_b, acc,
    xo, xt, go, gt, so, st, ro, rt,
    load_sem, d_recv, g_send, g_recv, m_send, m_recv, w_send, w_recv, x_send, x_recv,
    q_send, q_recv, f_send, f_recv, o_send, o_recv, t_send, t_recv, ready,
):
    s, h = lax.axis_index("seq"), lax.axis_index("head")
    x, y, zl = lax.div(s, 32), lax.rem(lax.div(s, 8), 4), lax.rem(s, 8)
    zh, c = lax.div(h, 2), lax.rem(h, 2)
    p = lax.rem(zl, 2)
    near = lax.div(zl, 4)
    other = h + 1 - 2 * c
    across = lax.rem(h + 2, 4)
    column = s - zl
    mine = c == p

    def rdma(src, dst, send, recv, dev):
        return pltpu.make_async_remote_copy(
            src_ref=src, dst_ref=dst, send_sem=send, recv_sem=recv, device_id=dev, device_id_type=MESH
        )

    barrier = pltpu.get_barrier_semaphore()

    def plane(px, py):
        return ((px * 4 + py) * 8 + zl, h)

    def greet(dev):
        pl.semaphore_signal(barrier, inc=1, device_id=dev, device_id_type=MESH)

    q_self = jnp.logical_and(mine, near == c)

    swap_to = (s + 1 - 2 * p, other)

    @pl.when(jnp.logical_not(mine))
    def _():
        greet(swap_to)

    for n in (1, 3, 2):
        greet(plane(lax.rem(x + n, 4), y))
        greet(plane(x, lax.rem(y + n, 4)))
    greet((s, other))
    greet((s, across))
    for n in range(4):

        @pl.when(jnp.logical_not(jnp.logical_and(q_self, c * 4 + n == zl)))
        def _():
            greet((column + c * 4 + n, zh * 2 + p))

    loads = [
        pltpu.make_async_copy(src, dst, load_sem.at[i])
        for i, (src, dst) in enumerate(
            [
                (tok_hbm, tok),
                (wk_hbm, wkv.at[:, pl.ds(0, HD)]),
                (wv_hbm, wkv.at[:, pl.ds(HD, HD)]),
                (wq_hbm, wq),
                (wo_hbm, wall.at[pl.ds(pl.multiple_of(h * HD, HD), HD)]),
                (temper_hbm, temper),
            ]
        )
    ]
    for load in loads:
        load.start()

    acc[...] = jnp.zeros_like(acc)

    half_rows = ROWS // 2

    def rows_of(at, part):
        if part is None:
            return pl.ds(pl.multiple_of(at * half_rows, half_rows), half_rows)
        return pl.ds(pl.multiple_of(at * half_rows + part * PART, PART), PART)

    def a_view(px, py, part):
        return kv_a.at[rows_of(py * 4 + px, part)]

    def b_view(px, py, part):
        return kv_b.at[rows_of(px * 4 + py, part)]

    sems = (d_recv, g_send, g_recv)
    along_x = Gather(kvown.at[pl.ds(0, half_rows)], a_view, (x, y), True, 0, sems, plane)
    along_y = Gather(kvown.at[pl.ds(half_rows, half_rows)], b_view, (x, y), False, 1, sems, plane)
    gathers = (along_x, along_y)

    def head_rows(head):
        return wall.at[pl.ds(pl.multiple_of(head * HD, HD), HD)]

    def w_piece(head, px):
        first = pl.multiple_of(head * HD + lax.rem(px, 2) * 64, 64)
        lanes = pl.multiple_of((y * 2 + lax.div(px, 2)) * 128, 128)
        return wall.at[pl.ds(first, 64), pl.ds(lanes, 128)]

    def w_row(head, py):
        return wall.at[pl.ds(pl.multiple_of(head * HD, HD), HD), pl.ds(pl.multiple_of(py * 256, 256), 256)]

    def w_share_x(n, received=False):
        ref = w_piece(across, lax.rem(x + 4 - n, 4) if received else x)
        return rdma(ref, ref, w_send.at[0], w_recv.at[n], plane(lax.rem(x + n, 4), y))

    def w_share_y(n, received=False):
        ref = w_row(across, lax.rem(y + 4 - n, 4) if received else y)
        return rdma(ref, ref, w_send.at[1], w_recv.at[4 + n], plane(x, lax.rem(y + n, 4)))

    w_across = rdma(w_piece(h, x), w_piece(h, x), m_send.at[0], m_recv.at[0], (s, across))
    w_across_in = rdma(w_piece(across, x), w_piece(across, x), m_send.at[0], m_recv.at[0], (s, across))
    w_other = rdma(head_rows(h), head_rows(h), m_send.at[1], m_recv.at[1], (s, other))
    w_other_in = rdma(head_rows(other), head_rows(other), m_send.at[1], m_recv.at[1], (s, other))
    far_other = lax.rem(other + 2, 4)
    w_last = rdma(head_rows(across), head_rows(across), m_send.at[2], m_recv.at[2], (s, other))
    w_last_in = rdma(head_rows(far_other), head_rows(far_other), m_send.at[2], m_recv.at[2], (s, other))

    loads[0].wait()
    loads[1].wait()
    loads[2].wait()
    raw = jnp.dot(tok[...], wkv[...], preferred_element_type=F32)
    both = jnp.concatenate([unit_rows(raw[:, :HD]), raw[:, HD:].astype(BF16)], axis=1)
    kv_swap = rdma(kvst, kvown, m_send.at[3], m_recv.at[3], swap_to)

    def give_first():
        for g in gathers:
            for n in (1, 3, 2):
                g.first(n).start()
        for g in gathers:
            g.start(0, 1)

    def place_own(block):
        kv_a[rows_of(y * 4 + x, None)] = block[:half_rows]
        kv_b[rows_of(x * 4 + y, None)] = block[half_rows:]

    @pl.when(mine)
    def _():
        kvown[...] = both
        place_own(both)
        pl.semaphore_wait(barrier, 12 - jnp.where(near == c, 1, 0))
        give_first()

    @pl.when(jnp.logical_not(mine))
    def _():
        kvst[...] = both
        pl.semaphore_wait(barrier, 13)
        kv_swap.start()

    loads[4].wait()
    w_across.start()
    loads[3].wait()
    query_unit = unit_rows(jnp.dot(tok[...], wq[...], preferred_element_type=F32))
    qst[...] = query_unit

    def q_view(u):
        return qbuf.at[pl.ds(pl.multiple_of(u * ROWS, ROWS), ROWS)]

    half, bit = lax.div(zl, 4), lax.rem(lax.div(zl, 2), 2)
    q_targets = (half * 2 + bit, half * 2 + 1 - bit, 2 - half * 2 + bit, 3 - half * 2 - bit)

    def q_copy(n):
        return rdma(
            qst,
            q_view(zl),
            q_send.at[n],
            q_recv.at[lax.rem(zl, 4)],
            (column + c + 2 * q_targets[n], zh * 2 + near),
        )

    @pl.when(q_self)
    def _():
        qbuf[pl.ds(pl.multiple_of(zl * ROWS, ROWS), ROWS)] = query_unit

    @pl.when(jnp.logical_not(q_self))
    def _():
        q_copy(0).start()

    q_copy(1).start()
    loads[5].wait()
    w_other.start()

    @pl.when(jnp.logical_not(mine))
    def _():
        kv_swap.wait_recv()
        place_own(kvown[...])
        give_first()

    for t, i in ((1, -1), (2, 1), (3, 2)):
        for g in gathers:
            g.first_got(i)
            g.start(4 * t, 4 * t + 1)

    for n in (2, 3):
        q_copy(n).start()

    def relay(g, t):
        g.got(4 * t)
        g.start(4 * t + 2)
        g.got(4 * t + 1)
        g.start(4 * t + 3)

    def unit_at(k):
        return k + near * (7 - 2 * k)

    def q_arrived(k):
        u = unit_at(k)
        slot = lax.rem(u, 4)
        first_core = (near == c) if k < 4 else (near != c)
        forward = rdma(q_view(u), q_view(u), f_send.at[slot], f_recv.at[slot], (s, other))
        direct = rdma(q_view(u), q_view(u), q_send.at[0], q_recv.at[slot], (s, other))

        @pl.when(first_core)
        def _():
            if k < 4:

                @pl.when(jnp.logical_not(jnp.logical_and(q_self, u == zl)))
                def _():
                    direct.wait_recv()
            else:
                direct.wait_recv()
            forward.start()

        @pl.when(jnp.logical_not(first_core))
        def _():
            forward.wait_recv()

    scale = temper[zh * 2 + p] * F32(math.log2(math.e) / math.sqrt(HD))

    ones = jnp.ones((4 * ROWS, HD), BF16)

    def piece(half, d):
        q0 = pl.multiple_of(half * (4 * ROWS), 4 * ROWS)
        a0 = pl.multiple_of(lax.rem(y + d, 4) * (2 * ROWS), 2 * ROWS)
        b0 = pl.multiple_of(lax.rem(x + d, 4) * (2 * ROWS), 2 * ROWS)
        both_k = jnp.concatenate([kv_a[pl.ds(a0, 2 * ROWS), :HD], kv_b[pl.ds(b0, 2 * ROWS), :HD]], axis=0)
        both_v = jnp.concatenate([kv_a[pl.ds(a0, 2 * ROWS), HD:], kv_b[pl.ds(b0, 2 * ROWS), HD:]], axis=0)
        score = lax.dot_general(
            qbuf[pl.ds(q0, 4 * ROWS)], both_k, (((1,), (1,)), ((), ())), preferred_element_type=F32
        )
        weight = jnp.exp2(score * scale).astype(BF16)
        value_block = jnp.concatenate([both_v, ones], axis=1)
        acc[pl.ds(q0, 4 * ROWS)] += jnp.dot(weight, value_block, preferred_element_type=F32)

    lane = lax.broadcasted_iota(jnp.int32, (PART, HD), 1)
    row = lax.broadcasted_iota(jnp.int32, (PART, HD), 0)
    diagonal = lane == row
    slot = (zh * 2 + p) * 4 + lax.div(zl, 2)

    def part_rows(core, i):
        return pl.ds(pl.multiple_of(core * (4 * ROWS) + i * PART, PART), PART)

    def give_copies(n):
        at = pl.ds(pl.multiple_of(n * 4, 4), 4)
        return (
            rdma(xo.at[at], go.at[at], x_send.at[0], x_recv.at[n], (s, other)),
            rdma(xt.at[at], gt.at[at], x_send.at[1], x_recv.at[4 + n], (s, other)),
        )

    def block_of(core, i):
        block = acc[part_rows(core, i)]
        return block[:, :HD], jnp.sum(jnp.where(diagonal, block[:, HD:], 0.0), axis=0, keepdims=True)

    def turn(n):
        return lax.rem(n + zl, 4)

    def give(m, carry):
        n = turn(m)

        def one(k, inner):
            i = n * 4 + k
            summed, xt[i] = block_of(1 - c, i)
            xo[i] = summed.astype(BF16)
            return inner

        lax.fori_loop(0, 4, one, 0)
        for copy in give_copies(n):
            copy.start()
        return carry

    def o_copy(i):
        dev = (column + c * 4 + lax.div(i, 4), lax.rem(i, 4))
        return (
            rdma(so.at[i], ro.at[slot], o_send, o_recv, dev),
            rdma(st.at[i], rt.at[slot], t_send, t_recv, dev),
        )

    def o_self(i):
        return jnp.logical_and(c * 4 + lax.div(i, 4) == zl, lax.rem(i, 4) == h)

    def settle(m, carry):
        n = turn(m)
        for copy in give_copies(n):
            copy.wait_recv()

        def one(k, inner):
            i = n * 4 + k
            summed, total = block_of(c, i)
            summed, total = (summed + go[i].astype(F32)).astype(BF16), total + gt[i]
            so[i], st[i] = summed, total

            @pl.when(o_self(i))
            def _():
                ro[slot], rt[slot] = summed, total

            @pl.when(jnp.logical_not(o_self(i)))
            def _():
                for copy in o_copy(i):
                    copy.start()

            return inner

        lax.fori_loop(0, 4, one, 0)
        return carry

    def step(i, carry):
        def at(n, events):
            @pl.when(i == n)
            def _():
                events()

        def before_1():
            for t in (1, 2, 3):
                for g in gathers:
                    relay(g, t)
            w_across_in.wait_recv()
            for n in (1, 3, 2):
                w_share_x(n).start()

        def before_3():
            for k in range(4, 8):
                q_arrived(k)
            pl.semaphore_signal(ready, inc=1, device_id=(s, across), device_id_type=MESH)
            for n in (1, 3, 2):
                w_share_x(n, True).wait_recv()
            for n in (1, 3, 2):
                w_share_y(n).start()

        def before_5():
            for n in (1, 3, 2):
                w_share_y(n, True).wait_recv()

        def before_6():
            for g in gathers:
                g.got(2, 3, 6, 7, 10, 11, 14, 15)

        def before_7():
            lax.fori_loop(0, 4, give, 0)

        at(1, before_1)
        at(3, before_3)
        at(5, before_5)
        at(6, before_6)
        at(7, before_7)
        near_now = jnp.logical_or(i < 3, i == jnp.where(near == c, 7, 6))
        r = jnp.where(i >= 6, 3, lax.rem(i, 3))
        piece(
            jnp.where(near_now, near, 1 - near),
            jnp.where(r == 0, 0, jnp.where(r == 1, 3, jnp.where(r == 2, 1, 2))),
        )
        return carry

    for g in gathers:
        relay(g, 0)
    for k in range(4):
        q_arrived(k)
    lax.fori_loop(0, 8, step, 0)

    w_last.start()
    pl.semaphore_wait(ready, 1)
    lax.fori_loop(0, 4, settle, 0)

    for g, ref in ((along_x, kv_a), (along_y, kv_b)):
        g.sent(ref.at[pl.ds(0, 15 * half_rows)])

    @pl.when(jnp.logical_not(mine))
    def _():
        kv_swap.wait_send()

    for copy in (w_across, w_other, w_last):
        copy.wait_send()
    three_pieces = wall.at[pl.ds(0, 64), pl.ds(0, 384)]
    three_rows = wall.at[pl.ds(0, HD), pl.ds(0, 768)]
    rdma(three_pieces, three_pieces, w_send.at[0], w_recv.at[1], plane(lax.rem(x + 1, 4), y)).wait_send()
    rdma(three_rows, three_rows, w_send.at[1], w_recv.at[5], plane(x, lax.rem(y + 1, 4))).wait_send()
    rdma(xo, go, x_send.at[0], x_recv.at[0], (s, other)).wait_send()
    rdma(xt, gt, x_send.at[1], x_recv.at[4], (s, other)).wait_send()

    @pl.when(jnp.logical_not(q_self))
    def _():
        q_copy(0).wait_send()

    for n in (1, 2, 3):
        q_copy(n).wait_send()

    def forwarded(i, carry):
        rdma(q_view(c * 4 + i), q_view(c * 4 + i), f_send.at[i], f_recv.at[i], (s, other)).wait_send()
        return carry

    lax.fori_loop(0, 4, forwarded, 0)

    w_other_in.wait_recv()
    w_last_in.wait_recv()

    def all_parts(count):
        at = pl.ds(0, count)
        return (
            rdma(so.at[at], ro.at[at], o_send, o_recv, (s, other)),
            rdma(st.at[at], rt.at[at], t_send, t_recv, (s, other)),
        )

    @pl.when(near == c)
    def _():
        for copy in all_parts(15):
            copy.wait_recv()

    @pl.when(near != c)
    def _():
        for copy in all_parts(16):
            copy.wait_recv()

    attended = []
    for head in range(4):
        summed = sum(ro[head * 4 + j].astype(F32) for j in range(4))
        total = sum(rt[head * 4 + j] for j in range(4))
        total = jnp.sum(jnp.where(diagonal, jnp.broadcast_to(total, (PART, HD)), 0.0), axis=1, keepdims=True)
        attended.append((summed / total).astype(BF16))
    out_ref[...] = jnp.dot(
        jnp.concatenate(attended, axis=1), wall[...], preferred_element_type=F32
    ).astype(BF16)

    @pl.when(near == c)
    def _():
        for copy in all_parts(15):
            copy.wait_send()

    @pl.when(near != c)
    def _():
        for copy in all_parts(16):
            copy.wait_send()


def on_device(tokens, w_query, w_key, w_value, w_out, temper):
    dma = pltpu.SemaphoreType.DMA
    args = [
        pltpu.with_memory_space_constraint(a, pltpu.HBM)
        for a in (tokens, w_query, w_key, w_value, w_out, temper)
    ]
    d_model = tokens.shape[1]
    return pl.pallas_call(
        kernel,
        out_shape=jax.ShapeDtypeStruct((PART, d_model), BF16),
        in_specs=[pl.BlockSpec(memory_space=pltpu.HBM)] * 6,
        out_specs=pl.BlockSpec(memory_space=pltpu.VMEM),
        scratch_shapes=[
            pltpu.SMEM((4,), F32),
            pltpu.VMEM((ROWS, d_model), BF16),
            pltpu.VMEM((d_model, HD), BF16),
            pltpu.VMEM((d_model, 2 * HD), BF16),
            pltpu.VMEM((4 * HD, d_model), BF16),
            pltpu.VMEM((ROWS, HD), BF16),
            pltpu.VMEM((ROWS, 2 * HD), BF16),
            pltpu.VMEM((ROWS, 2 * HD), BF16),
            pltpu.VMEM((NZ * ROWS, HD), BF16),
            pltpu.VMEM((8 * ROWS, 2 * HD), BF16),
            pltpu.VMEM((8 * ROWS, 2 * HD), BF16),
            pltpu.VMEM((NZ * ROWS, 2 * HD), F32),
            pltpu.VMEM((16, PART, HD), BF16),
            pltpu.VMEM((16, 1, HD), F32),
            pltpu.VMEM((16, PART, HD), BF16),
            pltpu.VMEM((16, 1, HD), F32),
            pltpu.VMEM((16, PART, HD), BF16),
            pltpu.VMEM((16, 1, HD), F32),
            pltpu.VMEM((16, PART, HD), BF16),
            pltpu.VMEM((16, 1, HD), F32),
            dma((6,)),
            dma((8,)),
            dma((2,)),
            dma((32,)),
            dma((4,)),
            dma((4,)),
            dma((2,)),
            dma((8,)),
            dma((2,)),
            dma((8,)),
            dma((4,)),
            dma((4,)),
            dma((4,)),
            dma((4,)),
            dma(()),
            dma(()),
            dma(()),
            dma(()),
            pltpu.SemaphoreType.REGULAR,
        ],
        compiler_params=pltpu.CompilerParams(
            collective_id=0, has_side_effects=True, vmem_limit_bytes=40 * 1024 * 1024
        ),
        name="layer",
    )(*args)


def solution(mesh):
    return jax.shard_map(
        on_device,
        mesh=mesh,
        in_specs=(
            P("seq", None),
            P(None, "head"),
            P(None, "head"),
            P(None, "head"),
            P("head", None),
            P(),
        ),
        out_specs=P(("seq", "head"), None),
        check_vma=False,
    )
```

```python
import functools
import math

import jax
import jax.numpy as jnp
from jax import lax
from jax.experimental import pallas as pl
from jax.experimental.pallas import tpu as pltpu
from jax.sharding import PartitionSpec as P

MESH = pl.DeviceIdType.MESH
HD = 128
EPS = 1e-06
ROWS = 192
PART = 48
NZ = 8
F32 = jnp.float32
BF16 = jnp.bfloat16


def unit_rows(raw):
    return (raw * lax.rsqrt(jnp.mean(raw * raw, axis=-1, keepdims=True) + EPS)).astype(BF16)


class Gather:
    ORDER = (0, -1, 1, 2)

    def __init__(self, own, view, place, x_first, number, sems, target):
        self.own, self.view, self.place, self.x_first, self.number = own, view, place, x_first, number
        self.d_recv, self.send_sem, self.recv_sem = sems
        self.target = target
        self.table = []
        for i in self.ORDER:
            self.table += [(i, 0, None, 1), (i, 0, None, -1), (i, -1, 0, 1), (i, 1, 1, -1)]

    def at(self, i, j):
        x, y = self.place
        dx, dy = (i, j) if self.x_first else (j, i)
        return lax.rem(x + dx + 8, 4), lax.rem(y + dy + 8, 4)

    def first(self, n, received=False):
        at = self.at(-n, 0) if received else self.place
        return pltpu.make_async_remote_copy(
            src_ref=self.own,
            dst_ref=self.view(*at, None),
            send_sem=self.send_sem.at[self.number],
            recv_sem=self.d_recv.at[self.number * 4 + n],
            device_id=self.target(*self.at(n, 0)),
            device_id_type=MESH,
        )

    def copy(self, k, received):
        i, j, part, step = self.table[k]
        ref = self.view(*self.at(i, j - step if received else j), part)
        return self.along(k, ref, self.at(0, step))

    def along(self, k, ref, to):
        return pltpu.make_async_remote_copy(
            src_ref=ref,
            dst_ref=ref,
            send_sem=self.send_sem.at[self.number],
            recv_sem=self.recv_sem.at[self.number * 16 + k],
            device_id=self.target(*to),
            device_id_type=MESH,
        )

    def first_got(self, i):
        self.first((-i) % 4, True).wait_recv()

    def start(self, *ks):
        for k in ks:
            self.copy(k, False).start()

    def got(self, *ks):
        for k in ks:
            self.copy(k, True).wait_recv()

    def sent(self, ref):
        self.along(0, ref, self.at(0, 1)).wait_send()


def kernel(
    tok_hbm, wq_hbm, wk_hbm, wv_hbm, wo_hbm, temper_hbm, out_ref,
    temper, tok, wq, wkv, wall, qst, kvst, kvown, qbuf, kv_a, kv_b, acc,
    xo, xt, go, gt, so, st, ro, rt,
    load_sem, d_recv, g_send, g_recv, m_send, m_recv, w_send, w_recv, x_send, x_recv,
    q_send, q_recv, f_send, f_recv, o_send, o_recv, t_send, t_recv, ready,
):
    s, h = lax.axis_index("seq"), lax.axis_index("head")
    x, y, zl = lax.div(s, 32), lax.rem(lax.div(s, 8), 4), lax.rem(s, 8)
    zh, c = lax.div(h, 2), lax.rem(h, 2)
    p = lax.rem(zl, 2)
    near = lax.div(zl, 4)
    other = h + 1 - 2 * c
    across = lax.rem(h + 2, 4)
    column = s - zl
    mine = c == p

    def rdma(src, dst, send, recv, dev):
        return pltpu.make_async_remote_copy(
            src_ref=src, dst_ref=dst, send_sem=send, recv_sem=recv, device_id=dev, device_id_type=MESH
        )

    barrier = pltpu.get_barrier_semaphore()

    def plane(px, py):
        return ((px * 4 + py) * 8 + zl, h)

    def greet(dev):
        pl.semaphore_signal(barrier, inc=1, device_id=dev, device_id_type=MESH)

    q_self = jnp.logical_and(mine, near == c)

    swap_to = (s + 1 - 2 * p, other)

    @pl.when(jnp.logical_not(mine))
    def _():
        greet(swap_to)

    for n in (1, 3, 2):
        greet(plane(lax.rem(x + n, 4), y))
        greet(plane(x, lax.rem(y + n, 4)))
    greet((s, other))
    greet((s, across))
    for n in range(4):

        @pl.when(jnp.logical_not(jnp.logical_and(q_self, c * 4 + n == zl)))
        def _():
            greet((column + c * 4 + n, zh * 2 + p))

    loads = [
        pltpu.make_async_copy(src, dst, load_sem.at[i])
        for i, (src, dst) in enumerate(
            [
                (tok_hbm, tok),
                (wk_hbm, wkv.at[:, pl.ds(0, HD)]),
                (wv_hbm, wkv.at[:, pl.ds(HD, HD)]),
                (wq_hbm, wq),
                (wo_hbm, wall.at[pl.ds(pl.multiple_of(h * HD, HD), HD)]),
                (temper_hbm, temper),
            ]
        )
    ]
    for load in loads:
        load.start()

    acc[...] = jnp.zeros_like(acc)

    half_rows = ROWS // 2

    def rows_of(at, part):
        if part is None:
            return pl.ds(pl.multiple_of(at * half_rows, half_rows), half_rows)
        return pl.ds(pl.multiple_of(at * half_rows + part * PART, PART), PART)

    def a_view(px, py, part):
        return kv_a.at[rows_of(py * 4 + px, part)]

    def b_view(px, py, part):
        return kv_b.at[rows_of(px * 4 + py, part)]

    sems = (d_recv, g_send, g_recv)
    along_x = Gather(kvown.at[pl.ds(0, half_rows)], a_view, (x, y), True, 0, sems, plane)
    along_y = Gather(kvown.at[pl.ds(half_rows, half_rows)], b_view, (x, y), False, 1, sems, plane)
    gathers = (along_x, along_y)

    def head_rows(head):
        return wall.at[pl.ds(pl.multiple_of(head * HD, HD), HD)]

    def w_piece(head, px):
        first = pl.multiple_of(head * HD + lax.rem(px, 2) * 64, 64)
        lanes = pl.multiple_of((y * 2 + lax.div(px, 2)) * 128, 128)
        return wall.at[pl.ds(first, 64), pl.ds(lanes, 128)]

    def w_row(head, py):
        return wall.at[pl.ds(pl.multiple_of(head * HD, HD), HD), pl.ds(pl.multiple_of(py * 256, 256), 256)]

    def w_share_x(n, received=False):
        ref = w_piece(across, lax.rem(x + 4 - n, 4) if received else x)
        return rdma(ref, ref, w_send.at[0], w_recv.at[n], plane(lax.rem(x + n, 4), y))

    def w_share_y(n, received=False):
        ref = w_row(across, lax.rem(y + 4 - n, 4) if received else y)
        return rdma(ref, ref, w_send.at[1], w_recv.at[4 + n], plane(x, lax.rem(y + n, 4)))

    w_across = rdma(w_piece(h, x), w_piece(h, x), m_send.at[0], m_recv.at[0], (s, across))
    w_across_in = rdma(w_piece(across, x), w_piece(across, x), m_send.at[0], m_recv.at[0], (s, across))
    w_other = rdma(head_rows(h), head_rows(h), m_send.at[1], m_recv.at[1], (s, other))
    w_other_in = rdma(head_rows(other), head_rows(other), m_send.at[1], m_recv.at[1], (s, other))
    far_other = lax.rem(other + 2, 4)
    w_last = rdma(head_rows(across), head_rows(across), m_send.at[2], m_recv.at[2], (s, other))
    w_last_in = rdma(head_rows(far_other), head_rows(far_other), m_send.at[2], m_recv.at[2], (s, other))

    loads[0].wait()
    loads[1].wait()
    loads[2].wait()
    raw = jnp.dot(tok[...], wkv[...], preferred_element_type=F32)
    both = jnp.concatenate([unit_rows(raw[:, :HD]), raw[:, HD:].astype(BF16)], axis=1)
    kv_swap = rdma(kvst, kvown, m_send.at[3], m_recv.at[3], swap_to)

    def give_first():
        for g in gathers:
            for n in (1, 3, 2):
                g.first(n).start()
        for g in gathers:
            g.start(0, 1)

    def place_own(block):
        kv_a[rows_of(y * 4 + x, None)] = block[:half_rows]
        kv_b[rows_of(x * 4 + y, None)] = block[half_rows:]

    @pl.when(mine)
    def _():
        kvown[...] = both
        place_own(both)
        pl.semaphore_wait(barrier, 12 - jnp.where(near == c, 1, 0))
        give_first()

    @pl.when(jnp.logical_not(mine))
    def _():
        kvst[...] = both
        pl.semaphore_wait(barrier, 13)
        kv_swap.start()

    loads[4].wait()
    w_across.start()
    loads[3].wait()
    query_unit = unit_rows(jnp.dot(tok[...], wq[...], preferred_element_type=F32))
    qst[...] = query_unit

    def q_view(u):
        return qbuf.at[pl.ds(pl.multiple_of(u * ROWS, ROWS), ROWS)]

    half, bit = lax.div(zl, 4), lax.rem(lax.div(zl, 2), 2)
    q_targets = (half * 2 + bit, half * 2 + 1 - bit, 2 - half * 2 + bit, 3 - half * 2 - bit)

    def q_copy(n):
        return rdma(
            qst,
            q_view(zl),
            q_send.at[n],
            q_recv.at[lax.rem(zl, 4)],
            (column + c + 2 * q_targets[n], zh * 2 + near),
        )

    @pl.when(q_self)
    def _():
        qbuf[pl.ds(pl.multiple_of(zl * ROWS, ROWS), ROWS)] = query_unit

    @pl.when(jnp.logical_not(q_self))
    def _():
        q_copy(0).start()

    for n in (1, 2, 3):
        q_copy(n).start()
    loads[5].wait()
    w_other.start()

    @pl.when(jnp.logical_not(mine))
    def _():
        kv_swap.wait_recv()
        place_own(kvown[...])
        give_first()

    for t, i in ((1, -1), (2, 1), (3, 2)):
        for g in gathers:
            g.first_got(i)
            g.start(4 * t, 4 * t + 1)

    def relay(g, t):
        g.got(4 * t)
        g.start(4 * t + 2)
        g.got(4 * t + 1)
        g.start(4 * t + 3)

    def unit_at(k):
        return k + near * (7 - 2 * k)

    def q_arrived(k):
        u = unit_at(k)
        slot = lax.rem(u, 4)
        first_core = (near == c) if k < 4 else (near != c)
        forward = rdma(q_view(u), q_view(u), f_send.at[slot], f_recv.at[slot], (s, other))
        direct = rdma(q_view(u), q_view(u), q_send.at[0], q_recv.at[slot], (s, other))

        @pl.when(first_core)
        def _():
            if k < 4:

                @pl.when(jnp.logical_not(jnp.logical_and(q_self, u == zl)))
                def _():
                    direct.wait_recv()
            else:
                direct.wait_recv()
            forward.start()

        @pl.when(jnp.logical_not(first_core))
        def _():
            forward.wait_recv()

    scale = temper[zh * 2 + p] * F32(math.log2(math.e) / math.sqrt(HD))

    ones = jnp.ones((4 * ROWS, HD), BF16)

    def piece(half, d):
        q0 = pl.multiple_of(half * (4 * ROWS), 4 * ROWS)
        a0 = pl.multiple_of(lax.rem(y + d, 4) * (2 * ROWS), 2 * ROWS)
        b0 = pl.multiple_of(lax.rem(x + d, 4) * (2 * ROWS), 2 * ROWS)
        both_k = jnp.concatenate([kv_a[pl.ds(a0, 2 * ROWS), :HD], kv_b[pl.ds(b0, 2 * ROWS), :HD]], axis=0)
        both_v = jnp.concatenate([kv_a[pl.ds(a0, 2 * ROWS), HD:], kv_b[pl.ds(b0, 2 * ROWS), HD:]], axis=0)
        score = lax.dot_general(
            qbuf[pl.ds(q0, 4 * ROWS)], both_k, (((1,), (1,)), ((), ())), preferred_element_type=F32
        )
        weight = jnp.exp2(score * scale).astype(BF16)
        value_block = jnp.concatenate([both_v, ones], axis=1)
        acc[pl.ds(q0, 4 * ROWS)] += jnp.dot(weight, value_block, preferred_element_type=F32)

    lane = lax.broadcasted_iota(jnp.int32, (PART, HD), 1)
    row = lax.broadcasted_iota(jnp.int32, (PART, HD), 0)
    diagonal = lane == row
    slot = (zh * 2 + p) * 4 + lax.div(zl, 2)

    def part_rows(core, i):
        return pl.ds(pl.multiple_of(core * (4 * ROWS) + i * PART, PART), PART)

    def give_copies(n):
        at = pl.ds(pl.multiple_of(n * 4, 4), 4)
        return (
            rdma(xo.at[at], go.at[at], x_send.at[0], x_recv.at[n], (s, other)),
            rdma(xt.at[at], gt.at[at], x_send.at[1], x_recv.at[4 + n], (s, other)),
        )

    def block_of(core, i):
        block = acc[part_rows(core, i)]
        return block[:, :HD], jnp.sum(jnp.where(diagonal, block[:, HD:], 0.0), axis=0, keepdims=True)

    def turn(n):
        return lax.rem(n + zl, 4)

    def give(m, carry):
        n = turn(m)

        def one(k, inner):
            i = n * 4 + k
            summed, xt[i] = block_of(1 - c, i)
            xo[i] = summed.astype(BF16)
            return inner

        lax.fori_loop(0, 4, one, 0)
        for copy in give_copies(n):
            copy.start()
        return carry

    def o_copy(i):
        dev = (column + c * 4 + lax.div(i, 4), lax.rem(i, 4))
        return (
            rdma(so.at[i], ro.at[slot], o_send, o_recv, dev),
            rdma(st.at[i], rt.at[slot], t_send, t_recv, dev),
        )

    def o_self(i):
        return jnp.logical_and(c * 4 + lax.div(i, 4) == zl, lax.rem(i, 4) == h)

    def settle(m, carry):
        n = turn(m)
        for copy in give_copies(n):
            copy.wait_recv()

        def one(k, inner):
            i = n * 4 + k
            summed, total = block_of(c, i)
            summed, total = (summed + go[i].astype(F32)).astype(BF16), total + gt[i]
            so[i], st[i] = summed, total

            @pl.when(o_self(i))
            def _():
                ro[slot], rt[slot] = summed, total

            @pl.when(jnp.logical_not(o_self(i)))
            def _():
                for copy in o_copy(i):
                    copy.start()

            return inner

        lax.fori_loop(0, 4, one, 0)
        return carry

    def step(i, carry):
        def at(n, events):
            @pl.when(i == n)
            def _():
                events()

        def before_1():
            for t in (1, 2, 3):
                for g in gathers:
                    relay(g, t)
            w_across_in.wait_recv()
            for n in (1, 3, 2):
                w_share_x(n).start()

        def before_3():
            for k in range(4, 8):
                q_arrived(k)
            pl.semaphore_signal(ready, inc=1, device_id=(s, across), device_id_type=MESH)
            for n in (1, 3, 2):
                w_share_x(n, True).wait_recv()
            for n in (1, 3, 2):
                w_share_y(n).start()

        def before_5():
            for n in (1, 3, 2):
                w_share_y(n, True).wait_recv()

        def before_6():
            for g in gathers:
                g.got(2, 3, 6, 7, 10, 11, 14, 15)

        def before_7():
            lax.fori_loop(0, 4, give, 0)

        at(1, before_1)
        at(3, before_3)
        at(5, before_5)
        at(6, before_6)
        at(7, before_7)
        near_now = jnp.logical_or(i < 3, i == jnp.where(near == c, 7, 6))
        r = jnp.where(i >= 6, 3, lax.rem(i, 3))
        piece(
            jnp.where(near_now, near, 1 - near),
            jnp.where(r == 0, 0, jnp.where(r == 1, 3, jnp.where(r == 2, 1, 2))),
        )
        return carry

    for g in gathers:
        relay(g, 0)
    for k in range(4):
        q_arrived(k)
    lax.fori_loop(0, 8, step, 0)

    w_last.start()
    pl.semaphore_wait(ready, 1)
    lax.fori_loop(0, 4, settle, 0)

    for g, ref in ((along_x, kv_a), (along_y, kv_b)):
        g.sent(ref.at[pl.ds(0, 15 * half_rows)])

    @pl.when(jnp.logical_not(mine))
    def _():
        kv_swap.wait_send()

    for copy in (w_across, w_other, w_last):
        copy.wait_send()
    three_pieces = wall.at[pl.ds(0, 64), pl.ds(0, 384)]
    three_rows = wall.at[pl.ds(0, HD), pl.ds(0, 768)]
    rdma(three_pieces, three_pieces, w_send.at[0], w_recv.at[1], plane(lax.rem(x + 1, 4), y)).wait_send()
    rdma(three_rows, three_rows, w_send.at[1], w_recv.at[5], plane(x, lax.rem(y + 1, 4))).wait_send()
    rdma(xo, go, x_send.at[0], x_recv.at[0], (s, other)).wait_send()
    rdma(xt, gt, x_send.at[1], x_recv.at[4], (s, other)).wait_send()

    @pl.when(jnp.logical_not(q_self))
    def _():
        q_copy(0).wait_send()

    for n in (1, 2, 3):
        q_copy(n).wait_send()

    def forwarded(i, carry):
        rdma(q_view(c * 4 + i), q_view(c * 4 + i), f_send.at[i], f_recv.at[i], (s, other)).wait_send()
        return carry

    lax.fori_loop(0, 4, forwarded, 0)

    w_other_in.wait_recv()
    w_last_in.wait_recv()

    def all_parts(count):
        at = pl.ds(0, count)
        return (
            rdma(so.at[at], ro.at[at], o_send, o_recv, (s, other)),
            rdma(st.at[at], rt.at[at], t_send, t_recv, (s, other)),
        )

    @pl.when(near == c)
    def _():
        for copy in all_parts(15):
            copy.wait_recv()

    @pl.when(near != c)
    def _():
        for copy in all_parts(16):
            copy.wait_recv()

    attended = []
    for head in range(4):
        summed = sum(ro[head * 4 + j].astype(F32) for j in range(4))
        total = sum(rt[head * 4 + j] for j in range(4))
        total = jnp.sum(jnp.where(diagonal, jnp.broadcast_to(total, (PART, HD)), 0.0), axis=1, keepdims=True)
        attended.append((summed / total).astype(BF16))
    out_ref[...] = jnp.dot(
        jnp.concatenate(attended, axis=1), wall[...], preferred_element_type=F32
    ).astype(BF16)

    @pl.when(near == c)
    def _():
        for copy in all_parts(15):
            copy.wait_send()

    @pl.when(near != c)
    def _():
        for copy in all_parts(16):
            copy.wait_send()


def on_device(tokens, w_query, w_key, w_value, w_out, temper):
    dma = pltpu.SemaphoreType.DMA
    args = [
        pltpu.with_memory_space_constraint(a, pltpu.HBM)
        for a in (tokens, w_query, w_key, w_value, w_out, temper)
    ]
    d_model = tokens.shape[1]
    return pl.pallas_call(
        kernel,
        out_shape=jax.ShapeDtypeStruct((PART, d_model), BF16),
        in_specs=[pl.BlockSpec(memory_space=pltpu.HBM)] * 6,
        out_specs=pl.BlockSpec(memory_space=pltpu.VMEM),
        scratch_shapes=[
            pltpu.SMEM((4,), F32),
            pltpu.VMEM((ROWS, d_model), BF16),
            pltpu.VMEM((d_model, HD), BF16),
            pltpu.VMEM((d_model, 2 * HD), BF16),
            pltpu.VMEM((4 * HD, d_model), BF16),
            pltpu.VMEM((ROWS, HD), BF16),
            pltpu.VMEM((ROWS, 2 * HD), BF16),
            pltpu.VMEM((ROWS, 2 * HD), BF16),
            pltpu.VMEM((NZ * ROWS, HD), BF16),
            pltpu.VMEM((8 * ROWS, 2 * HD), BF16),
            pltpu.VMEM((8 * ROWS, 2 * HD), BF16),
            pltpu.VMEM((NZ * ROWS, 2 * HD), F32),
            pltpu.VMEM((16, PART, HD), BF16),
            pltpu.VMEM((16, 1, HD), F32),
            pltpu.VMEM((16, PART, HD), BF16),
            pltpu.VMEM((16, 1, HD), F32),
            pltpu.VMEM((16, PART, HD), BF16),
            pltpu.VMEM((16, 1, HD), F32),
            pltpu.VMEM((16, PART, HD), BF16),
            pltpu.VMEM((16, 1, HD), F32),
            dma((6,)),
            dma((8,)),
            dma((2,)),
            dma((32,)),
            dma((4,)),
            dma((4,)),
            dma((2,)),
            dma((8,)),
            dma((2,)),
            dma((8,)),
            dma((4,)),
            dma((4,)),
            dma((4,)),
            dma((4,)),
            dma(()),
            dma(()),
            dma(()),
            dma(()),
            pltpu.SemaphoreType.REGULAR,
        ],
        compiler_params=pltpu.CompilerParams(
            collective_id=0, has_side_effects=True, vmem_limit_bytes=40 * 1024 * 1024
        ),
        name="layer",
    )(*args)


def solution(mesh):
    return jax.shard_map(
        on_device,
        mesh=mesh,
        in_specs=(
            P("seq", None),
            P(None, "head"),
            P(None, "head"),
            P(None, "head"),
            P("head", None),
            P(),
        ),
        out_specs=P(("seq", "head"), None),
        check_vma=False,
    )
```

```python
import functools
import math

import jax
import jax.numpy as jnp
from jax import lax
from jax.experimental import pallas as pl
from jax.experimental.pallas import tpu as pltpu
from jax.sharding import PartitionSpec as P

MESH = pl.DeviceIdType.MESH
HD = 128
EPS = 1e-06
ROWS = 192
PART = 48
NZ = 8
F32 = jnp.float32
BF16 = jnp.bfloat16


def unit_rows(raw):
    return (raw * lax.rsqrt(jnp.mean(raw * raw, axis=-1, keepdims=True) + EPS)).astype(BF16)


class Gather:
    ORDER = (0, -1, 1, 2)

    def __init__(self, own, view, place, x_first, number, sems, target):
        self.own, self.view, self.place, self.x_first, self.number = own, view, place, x_first, number
        self.d_recv, self.send_sem, self.recv_sem = sems
        self.target = target
        self.table = []
        for i in self.ORDER:
            self.table += [(i, 0, None, 1), (i, 0, None, -1), (i, -1, 0, 1), (i, 1, 1, -1)]

    def at(self, i, j):
        x, y = self.place
        dx, dy = (i, j) if self.x_first else (j, i)
        return lax.rem(x + dx + 8, 4), lax.rem(y + dy + 8, 4)

    def first(self, n, received=False):
        at = self.at(-n, 0) if received else self.place
        return pltpu.make_async_remote_copy(
            src_ref=self.own,
            dst_ref=self.view(*at, None),
            send_sem=self.send_sem.at[self.number],
            recv_sem=self.d_recv.at[self.number * 4 + n],
            device_id=self.target(*self.at(n, 0)),
            device_id_type=MESH,
        )

    def copy(self, k, received):
        i, j, part, step = self.table[k]
        ref = self.view(*self.at(i, j - step if received else j), part)
        return self.along(k, ref, self.at(0, step))

    def along(self, k, ref, to):
        return pltpu.make_async_remote_copy(
            src_ref=ref,
            dst_ref=ref,
            send_sem=self.send_sem.at[self.number],
            recv_sem=self.recv_sem.at[self.number * 16 + k],
            device_id=self.target(*to),
            device_id_type=MESH,
        )

    def first_got(self, i):
        self.first((-i) % 4, True).wait_recv()

    def start(self, *ks):
        for k in ks:
            self.copy(k, False).start()

    def got(self, *ks):
        for k in ks:
            self.copy(k, True).wait_recv()

    def sent(self, ref):
        self.along(0, ref, self.at(0, 1)).wait_send()


def kernel(
    tok_hbm, wq_hbm, wk_hbm, wv_hbm, wo_hbm, temper_hbm, out_ref,
    temper, tok, wq, wkv, wall, qst, kvst, kvown, qbuf, kv_a, kv_b, acc,
    xo, xt, go, gt, so, st, ro, rt,
    load_sem, d_recv, g_send, g_recv, m_send, m_recv, w_send, w_recv, x_send, x_recv,
    q_send, q_recv, f_send, f_recv, o_send, o_recv, t_send, t_recv, ready,
):
    s, h = lax.axis_index("seq"), lax.axis_index("head")
    x, y, zl = lax.div(s, 32), lax.rem(lax.div(s, 8), 4), lax.rem(s, 8)
    zh, c = lax.div(h, 2), lax.rem(h, 2)
    p = lax.rem(zl, 2)
    near = lax.div(zl, 4)
    other = h + 1 - 2 * c
    across = lax.rem(h + 2, 4)
    column = s - zl
    mine = c == p

    def rdma(src, dst, send, recv, dev):
        return pltpu.make_async_remote_copy(
            src_ref=src, dst_ref=dst, send_sem=send, recv_sem=recv, device_id=dev, device_id_type=MESH
        )

    barrier = pltpu.get_barrier_semaphore()

    def plane(px, py):
        return ((px * 4 + py) * 8 + zl, h)

    def greet(dev):
        pl.semaphore_signal(barrier, inc=1, device_id=dev, device_id_type=MESH)

    q_self = jnp.logical_and(mine, near == c)

    swap_to = (s + 1 - 2 * p, other)

    @pl.when(jnp.logical_not(mine))
    def _():
        greet(swap_to)

    for n in (1, 3, 2):
        greet(plane(lax.rem(x + n, 4), y))
        greet(plane(x, lax.rem(y + n, 4)))
    greet((s, other))
    greet((s, across))
    for n in range(4):

        @pl.when(jnp.logical_not(jnp.logical_and(q_self, c * 4 + n == zl)))
        def _():
            greet((column + c * 4 + n, zh * 2 + p))

    loads = [
        pltpu.make_async_copy(src, dst, load_sem.at[i])
        for i, (src, dst) in enumerate(
            [
                (tok_hbm, tok),
                (wk_hbm, wkv.at[:, pl.ds(0, HD)]),
                (wv_hbm, wkv.at[:, pl.ds(HD, HD)]),
                (wq_hbm, wq),
                (wo_hbm, wall.at[pl.ds(pl.multiple_of(h * HD, HD), HD)]),
                (temper_hbm, temper),
            ]
        )
    ]
    for load in loads:
        load.start()

    acc[...] = jnp.zeros_like(acc)

    half_rows = ROWS // 2

    def rows_of(at, part):
        if part is None:
            return pl.ds(pl.multiple_of(at * half_rows, half_rows), half_rows)
        return pl.ds(pl.multiple_of(at * half_rows + part * PART, PART), PART)

    def a_view(px, py, part):
        return kv_a.at[rows_of(py * 4 + px, part)]

    def b_view(px, py, part):
        return kv_b.at[rows_of(px * 4 + py, part)]

    sems = (d_recv, g_send, g_recv)
    along_x = Gather(kvown.at[pl.ds(0, half_rows)], a_view, (x, y), True, 0, sems, plane)
    along_y = Gather(kvown.at[pl.ds(half_rows, half_rows)], b_view, (x, y), False, 1, sems, plane)
    gathers = (along_x, along_y)

    def head_rows(head):
        return wall.at[pl.ds(pl.multiple_of(head * HD, HD), HD)]

    def w_piece(head, px):
        first = pl.multiple_of(head * HD + lax.rem(px, 2) * 64, 64)
        lanes = pl.multiple_of((y * 2 + lax.div(px, 2)) * 128, 128)
        return wall.at[pl.ds(first, 64), pl.ds(lanes, 128)]

    def w_row(head, py):
        return wall.at[pl.ds(pl.multiple_of(head * HD, HD), HD), pl.ds(pl.multiple_of(py * 256, 256), 256)]

    def w_share_x(n, received=False):
        ref = w_piece(across, lax.rem(x + 4 - n, 4) if received else x)
        return rdma(ref, ref, w_send.at[0], w_recv.at[n], plane(lax.rem(x + n, 4), y))

    def w_share_y(n, received=False):
        ref = w_row(across, lax.rem(y + 4 - n, 4) if received else y)
        return rdma(ref, ref, w_send.at[1], w_recv.at[4 + n], plane(x, lax.rem(y + n, 4)))

    w_across = rdma(w_piece(h, x), w_piece(h, x), m_send.at[0], m_recv.at[0], (s, across))
    w_across_in = rdma(w_piece(across, x), w_piece(across, x), m_send.at[0], m_recv.at[0], (s, across))
    w_other = rdma(head_rows(h), head_rows(h), m_send.at[1], m_recv.at[1], (s, other))
    w_other_in = rdma(head_rows(other), head_rows(other), m_send.at[1], m_recv.at[1], (s, other))
    far_other = lax.rem(other + 2, 4)
    w_last = rdma(head_rows(across), head_rows(across), m_send.at[2], m_recv.at[2], (s, other))
    w_last_in = rdma(head_rows(far_other), head_rows(far_other), m_send.at[2], m_recv.at[2], (s, other))

    loads[0].wait()
    loads[1].wait()
    loads[2].wait()
    raw = jnp.dot(tok[...], wkv[...], preferred_element_type=F32)
    both = jnp.concatenate([unit_rows(raw[:, :HD]), raw[:, HD:].astype(BF16)], axis=1)
    kv_swap = rdma(kvst, kvown, m_send.at[3], m_recv.at[3], swap_to)

    def give_first():
        for g in gathers:
            for n in (1, 3, 2):
                g.first(n).start()
        for g in gathers:
            g.start(0, 1)

    def place_own(block):
        kv_a[rows_of(y * 4 + x, None)] = block[:half_rows]
        kv_b[rows_of(x * 4 + y, None)] = block[half_rows:]

    @pl.when(mine)
    def _():
        kvown[...] = both
        place_own(both)
        pl.semaphore_wait(barrier, 12 - jnp.where(near == c, 1, 0))
        give_first()

    @pl.when(jnp.logical_not(mine))
    def _():
        kvst[...] = both
        pl.semaphore_wait(barrier, 13)
        kv_swap.start()

    loads[4].wait()
    w_across.start()
    loads[3].wait()
    query_unit = unit_rows(jnp.dot(tok[...], wq[...], preferred_element_type=F32))
    qst[...] = query_unit

    def q_view(u):
        return qbuf.at[pl.ds(pl.multiple_of(u * ROWS, ROWS), ROWS)]

    half, bit = lax.div(zl, 4), lax.rem(lax.div(zl, 2), 2)
    q_targets = (half * 2 + bit, half * 2 + 1 - bit, 2 - half * 2 + bit, 3 - half * 2 - bit)

    def q_copy(n):
        return rdma(
            qst,
            q_view(zl),
            q_send.at[n],
            q_recv.at[lax.rem(zl, 4)],
            (column + c + 2 * q_targets[n], zh * 2 + near),
        )

    @pl.when(q_self)
    def _():
        qbuf[pl.ds(pl.multiple_of(zl * ROWS, ROWS), ROWS)] = query_unit

    @pl.when(jnp.logical_not(q_self))
    def _():
        q_copy(0).start()

    for n in (1, 2, 3):
        q_copy(n).start()
    loads[5].wait()

    @pl.when(jnp.logical_not(mine))
    def _():
        kv_swap.wait_recv()
        place_own(kvown[...])
        give_first()

    for t, i in ((1, -1), (2, 1), (3, 2)):
        for g in gathers:
            g.first_got(i)
            g.start(4 * t, 4 * t + 1)

    def relay(g, t):
        g.got(4 * t)
        g.start(4 * t + 2)
        g.got(4 * t + 1)
        g.start(4 * t + 3)

    def unit_at(k):
        return k + near * (7 - 2 * k)

    def q_arrived(k):
        u = unit_at(k)
        slot = lax.rem(u, 4)
        first_core = (near == c) if k < 4 else (near != c)
        forward = rdma(q_view(u), q_view(u), f_send.at[slot], f_recv.at[slot], (s, other))
        direct = rdma(q_view(u), q_view(u), q_send.at[0], q_recv.at[slot], (s, other))

        @pl.when(first_core)
        def _():
            if k < 4:

                @pl.when(jnp.logical_not(jnp.logical_and(q_self, u == zl)))
                def _():
                    direct.wait_recv()
            else:
                direct.wait_recv()
            forward.start()

        @pl.when(jnp.logical_not(first_core))
        def _():
            forward.wait_recv()

    scale = temper[zh * 2 + p] * F32(math.log2(math.e) / math.sqrt(HD))

    ones = jnp.ones((4 * ROWS, HD), BF16)

    def piece(half, d):
        q0 = pl.multiple_of(half * (4 * ROWS), 4 * ROWS)
        a0 = pl.multiple_of(lax.rem(y + d, 4) * (2 * ROWS), 2 * ROWS)
        b0 = pl.multiple_of(lax.rem(x + d, 4) * (2 * ROWS), 2 * ROWS)
        both_k = jnp.concatenate([kv_a[pl.ds(a0, 2 * ROWS), :HD], kv_b[pl.ds(b0, 2 * ROWS), :HD]], axis=0)
        both_v = jnp.concatenate([kv_a[pl.ds(a0, 2 * ROWS), HD:], kv_b[pl.ds(b0, 2 * ROWS), HD:]], axis=0)
        score = lax.dot_general(
            qbuf[pl.ds(q0, 4 * ROWS)], both_k, (((1,), (1,)), ((), ())), preferred_element_type=F32
        )
        weight = jnp.exp2(score * scale).astype(BF16)
        value_block = jnp.concatenate([both_v, ones], axis=1)
        acc[pl.ds(q0, 4 * ROWS)] += jnp.dot(weight, value_block, preferred_element_type=F32)

    lane = lax.broadcasted_iota(jnp.int32, (PART, HD), 1)
    row = lax.broadcasted_iota(jnp.int32, (PART, HD), 0)
    diagonal = lane == row
    slot = (zh * 2 + p) * 4 + lax.div(zl, 2)

    def part_rows(core, i):
        return pl.ds(pl.multiple_of(core * (4 * ROWS) + i * PART, PART), PART)

    def give_copies(n):
        at = pl.ds(pl.multiple_of(n * 4, 4), 4)
        return (
            rdma(xo.at[at], go.at[at], x_send.at[0], x_recv.at[n], (s, other)),
            rdma(xt.at[at], gt.at[at], x_send.at[1], x_recv.at[4 + n], (s, other)),
        )

    def block_of(core, i):
        block = acc[part_rows(core, i)]
        return block[:, :HD], jnp.sum(jnp.where(diagonal, block[:, HD:], 0.0), axis=0, keepdims=True)

    def turn(n):
        return lax.rem(n + zl, 4)

    def give(m, carry):
        n = turn(m)

        def one(k, inner):
            i = n * 4 + k
            summed, xt[i] = block_of(1 - c, i)
            xo[i] = summed.astype(BF16)
            return inner

        lax.fori_loop(0, 4, one, 0)
        for copy in give_copies(n):
            copy.start()
        return carry

    def o_copy(i):
        dev = (column + c * 4 + lax.div(i, 4), lax.rem(i, 4))
        return (
            rdma(so.at[i], ro.at[slot], o_send, o_recv, dev),
            rdma(st.at[i], rt.at[slot], t_send, t_recv, dev),
        )

    def o_self(i):
        return jnp.logical_and(c * 4 + lax.div(i, 4) == zl, lax.rem(i, 4) == h)

    def settle(m, carry):
        n = turn(m)
        for copy in give_copies(n):
            copy.wait_recv()

        def one(k, inner):
            i = n * 4 + k
            summed, total = block_of(c, i)
            summed, total = (summed + go[i].astype(F32)).astype(BF16), total + gt[i]
            so[i], st[i] = summed, total

            @pl.when(o_self(i))
            def _():
                ro[slot], rt[slot] = summed, total

            @pl.when(jnp.logical_not(o_self(i)))
            def _():
                for copy in o_copy(i):
                    copy.start()

            return inner

        lax.fori_loop(0, 4, one, 0)
        return carry

    def step(i, carry):
        def at(n, events):
            @pl.when(i == n)
            def _():
                events()

        def before_1():
            for t in (1, 2, 3):
                for g in gathers:
                    relay(g, t)
            w_across_in.wait_recv()
            for n in (1, 3, 2):
                w_share_x(n).start()

        def before_3():
            for k in range(4, 8):
                q_arrived(k)
            pl.semaphore_signal(ready, inc=1, device_id=(s, across), device_id_type=MESH)
            for n in (1, 3, 2):
                w_share_x(n, True).wait_recv()
            for n in (1, 3, 2):
                w_share_y(n).start()

        def before_5():
            for n in (1, 3, 2):
                w_share_y(n, True).wait_recv()

        def before_6():
            for g in gathers:
                g.got(2, 3, 6, 7, 10, 11, 14, 15)

        def before_7():
            lax.fori_loop(0, 4, give, 0)

        at(1, before_1)
        at(3, before_3)
        at(5, before_5)
        at(6, before_6)
        at(7, before_7)
        near_now = jnp.logical_or(i < 3, i == jnp.where(near == c, 7, 6))
        r = jnp.where(i >= 6, 3, lax.rem(i, 3))
        piece(
            jnp.where(near_now, near, 1 - near),
            jnp.where(r == 0, 0, jnp.where(r == 1, 3, jnp.where(r == 2, 1, 2))),
        )
        return carry

    for g in gathers:
        relay(g, 0)
    for k in range(4):
        q_arrived(k)
    w_other.start()
    lax.fori_loop(0, 8, step, 0)

    w_last.start()
    pl.semaphore_wait(ready, 1)
    lax.fori_loop(0, 4, settle, 0)

    for g, ref in ((along_x, kv_a), (along_y, kv_b)):
        g.sent(ref.at[pl.ds(0, 15 * half_rows)])

    @pl.when(jnp.logical_not(mine))
    def _():
        kv_swap.wait_send()

    for copy in (w_across, w_other, w_last):
        copy.wait_send()
    three_pieces = wall.at[pl.ds(0, 64), pl.ds(0, 384)]
    three_rows = wall.at[pl.ds(0, HD), pl.ds(0, 768)]
    rdma(three_pieces, three_pieces, w_send.at[0], w_recv.at[1], plane(lax.rem(x + 1, 4), y)).wait_send()
    rdma(three_rows, three_rows, w_send.at[1], w_recv.at[5], plane(x, lax.rem(y + 1, 4))).wait_send()
    rdma(xo, go, x_send.at[0], x_recv.at[0], (s, other)).wait_send()
    rdma(xt, gt, x_send.at[1], x_recv.at[4], (s, other)).wait_send()

    @pl.when(jnp.logical_not(q_self))
    def _():
        q_copy(0).wait_send()

    for n in (1, 2, 3):
        q_copy(n).wait_send()

    def forwarded(i, carry):
        rdma(q_view(c * 4 + i), q_view(c * 4 + i), f_send.at[i], f_recv.at[i], (s, other)).wait_send()
        return carry

    lax.fori_loop(0, 4, forwarded, 0)

    w_other_in.wait_recv()
    w_last_in.wait_recv()

    def all_parts(count):
        at = pl.ds(0, count)
        return (
            rdma(so.at[at], ro.at[at], o_send, o_recv, (s, other)),
            rdma(st.at[at], rt.at[at], t_send, t_recv, (s, other)),
        )

    @pl.when(near == c)
    def _():
        for copy in all_parts(15):
            copy.wait_recv()

    @pl.when(near != c)
    def _():
        for copy in all_parts(16):
            copy.wait_recv()

    attended = []
    for head in range(4):
        summed = sum(ro[head * 4 + j].astype(F32) for j in range(4))
        total = sum(rt[head * 4 + j] for j in range(4))
        total = jnp.sum(jnp.where(diagonal, jnp.broadcast_to(total, (PART, HD)), 0.0), axis=1, keepdims=True)
        attended.append((summed / total).astype(BF16))
    out_ref[...] = jnp.dot(
        jnp.concatenate(attended, axis=1), wall[...], preferred_element_type=F32
    ).astype(BF16)

    @pl.when(near == c)
    def _():
        for copy in all_parts(15):
            copy.wait_send()

    @pl.when(near != c)
    def _():
        for copy in all_parts(16):
            copy.wait_send()


def on_device(tokens, w_query, w_key, w_value, w_out, temper):
    dma = pltpu.SemaphoreType.DMA
    args = [
        pltpu.with_memory_space_constraint(a, pltpu.HBM)
        for a in (tokens, w_query, w_key, w_value, w_out, temper)
    ]
    d_model = tokens.shape[1]
    return pl.pallas_call(
        kernel,
        out_shape=jax.ShapeDtypeStruct((PART, d_model), BF16),
        in_specs=[pl.BlockSpec(memory_space=pltpu.HBM)] * 6,
        out_specs=pl.BlockSpec(memory_space=pltpu.VMEM),
        scratch_shapes=[
            pltpu.SMEM((4,), F32),
            pltpu.VMEM((ROWS, d_model), BF16),
            pltpu.VMEM((d_model, HD), BF16),
            pltpu.VMEM((d_model, 2 * HD), BF16),
            pltpu.VMEM((4 * HD, d_model), BF16),
            pltpu.VMEM((ROWS, HD), BF16),
            pltpu.VMEM((ROWS, 2 * HD), BF16),
            pltpu.VMEM((ROWS, 2 * HD), BF16),
            pltpu.VMEM((NZ * ROWS, HD), BF16),
            pltpu.VMEM((8 * ROWS, 2 * HD), BF16),
            pltpu.VMEM((8 * ROWS, 2 * HD), BF16),
            pltpu.VMEM((NZ * ROWS, 2 * HD), F32),
            pltpu.VMEM((16, PART, HD), BF16),
            pltpu.VMEM((16, 1, HD), F32),
            pltpu.VMEM((16, PART, HD), BF16),
            pltpu.VMEM((16, 1, HD), F32),
            pltpu.VMEM((16, PART, HD), BF16),
            pltpu.VMEM((16, 1, HD), F32),
            pltpu.VMEM((16, PART, HD), BF16),
            pltpu.VMEM((16, 1, HD), F32),
            dma((6,)),
            dma((8,)),
            dma((2,)),
            dma((32,)),
            dma((4,)),
            dma((4,)),
            dma((2,)),
            dma((8,)),
            dma((2,)),
            dma((8,)),
            dma((4,)),
            dma((4,)),
            dma((4,)),
            dma((4,)),
            dma(()),
            dma(()),
            dma(()),
            dma(()),
            pltpu.SemaphoreType.REGULAR,
        ],
        compiler_params=pltpu.CompilerParams(
            collective_id=0, has_side_effects=True, vmem_limit_bytes=40 * 1024 * 1024
        ),
        name="layer",
    )(*args)


def solution(mesh):
    return jax.shard_map(
        on_device,
        mesh=mesh,
        in_specs=(
            P("seq", None),
            P(None, "head"),
            P(None, "head"),
            P(None, "head"),
            P("head", None),
            P(),
        ),
        out_specs=P(("seq", "head"), None),
        check_vma=False,
    )
```
